256 devices in a mesh: dp: 16 (over y, x_hi, core), space: 16 (over z, x_lo).
Axes of the slice: x: 4 (x_hi: 2, x_lo: 2; x = x_hi * 2 + x_lo), y: 4, z: 8, core: 2. Of those that a mesh axis runs over, the one named last changes fastest.
Arguments:
- features: bfloat16 [16, 64, 64, 512], P('dp', 'space'), may hold values from -45 to 45
- timestep: int32 [16], P('dp'), may hold values from 0 to 999
- w_time: bfloat16 [128, 512], replicated, may hold values from -0.5 to 0.5
- w_emb: bfloat16 [512, 1024], replicated, may hold values from -0.25 to 0.25
- w_qkv: bfloat16 [512, 1536], replicated, may hold values from -1.125 to 1.125
- w_out: bfloat16 [512, 512], replicated, may hold values from -0.25 to 0.25
- w_conv: bfloat16 [4608, 512], replicated, may hold values from -0.09375 to 0.09375
- upstream: bfloat16 [16, 64, 64, 512], P('dp', 'space'), may hold values from -6 to 6
Outputs:
- output: bfloat16 [16, 64, 64, 512], P('dp', 'space')
- grad_features: bfloat16 [16, 64, 64, 512], P('dp', 'space')
- grad_conv: float32 [2359296], P(('dp', 'space'))
- grad_out: float32 [262144], P(('dp', 'space'))
The draws below stay inside these ranges and needn't reach their ends.
All inputs are finite; a program needn't handle non-finite values.
Results may differ from the reference program's by a relative error of at most 0.015.
The reference program's roundings to bfloat16 on the way count: a program that leaves them out, or rounds other values in their place, can miss the bound.
Values may be sent and summed in bfloat16 or wider, within the bound.
A program may use at most 128 MiB of HBM per device.

```python
import math
import jax
import jax.numpy as jnp
from jax import lax

C = 512
HEADS = 8
HEAD_DIM = 64
GROUPS = 32
TFEAT = 128
EMB = 512
SIDE = 64
IMAGES = 16


def draw_features(key, part):
    key = jax.random.fold_in(key, 11)
    first_key, second_key, third_key = jax.random.split(key, 3)
    shape = (IMAGES, SIDE, SIDE, C)
    rows = jnp.arange(SIDE, dtype=jnp.float32) / (SIDE - 1)
    rise = 1.0 + 2.0 * rows
    offset = jax.random.uniform(first_key, (C,), jnp.float32, -1.0, 1.0)
    scales = jnp.exp(jax.random.uniform(second_key, (IMAGES, SIDE, SIDE, 1), jnp.float32, math.log(0.5), math.log(2.0)))
    noise = jax.random.truncated_normal(third_key, -4.0, 4.0, shape, jnp.float32)
    values = rise[None, :, None, None] * (offset[None, None, None, :] + scales * noise)
    return values.astype(jnp.bfloat16)


def draw_w_qkv(key, part):
    key = jax.random.fold_in(key, 23)
    first_key, second_key, third_key = jax.random.split(key, 3)
    factor = 1.0 / math.sqrt(C)
    queries = jax.random.truncated_normal(first_key, -4.0, 4.0, (C, C), jnp.float32) * factor
    values = jax.random.truncated_normal(third_key, -4.0, 4.0, (C, C), jnp.float32) * factor
    other = jax.random.truncated_normal(second_key, -4.0, 4.0, (C, C), jnp.float32) * factor
    keys = other
    return jnp.concatenate([queries, keys, values], axis=1).astype(jnp.bfloat16)


def touch_ends(values, key, least, top_value):
    index_at = [jax.random.randint(jax.random.fold_in(key, axis), (), 0, length) for axis, length in enumerate(values.shape)]
    longest = values.shape.index(max(values.shape))
    neighbour = index_at[:longest] + [(index_at[longest] + 1) % values.shape[longest]] + index_at[longest + 1:]
    return values.at[tuple(index_at)].set(least).at[tuple(neighbour)].set(top_value)


def shard_levels(rng, dims, cuts, smallest, high):
    factor_of, own = 1.0, jax.random.fold_in(rng, 6)
    for dim, shards_of in cuts:
        heights = jnp.exp(jax.random.uniform(jax.random.fold_in(own, dim), (shards_of,), jnp.float32, smallest / len(cuts), high / len(cuts)))
        factor_of = factor_of * jnp.repeat(heights, dims[dim] // shards_of).reshape([-1 if axis == dim else 1 for axis in range(len(dims))])
    return factor_of


def scatter_about(key, shape, scale, reach, shards=(), kind=jnp.bfloat16):
    array = scale * jax.random.normal(key, shape, jnp.float32)
    if shards:
        array = array * shard_levels(key, shape, shards, -0.22, 0.18)
    return jnp.clip(array, -reach, reach).astype(kind)


def setup_inputs(seed: int = 0) -> dict:
    streams_of = jax.random.split(jax.random.key(seed), 9)
    features = draw_features(jax.random.fold_in(streams_of[8], 71), 0)
    timestep = touch_ends(jax.random.randint(streams_of[1], (IMAGES,), 0, 1000), jax.random.fold_in(streams_of[1], 1), 0, 999).astype(jnp.int32)
    w_time = scatter_about(streams_of[2], (TFEAT, EMB), TFEAT ** -0.5, 0.5)
    w_emb = scatter_about(streams_of[3], (EMB, 2 * C), EMB ** -0.5, 0.25)
    w_qkv = draw_w_qkv(jax.random.fold_in(streams_of[8], 71), 0)
    w_out = scatter_about(streams_of[5], (C, C), C ** -0.5, 0.25)
    w_conv = scatter_about(streams_of[6], (9 * C, C), (9 * C) ** -0.5, 0.09375)
    upstream = scatter_about(streams_of[7], (IMAGES, SIDE, SIDE, C), 1.0, 6.0, ((0, 16), (1, 16)))
    return {"features": features, "timestep": timestep, "w_time": w_time, "w_emb": w_emb, "w_qkv": w_qkv, "w_out": w_out, "w_conv": w_conv, "upstream": upstream}


epsilon = 1e-05

def normalize(values):
    height, across, width = values.shape
    grouped = values.reshape(height * across, GROUPS, width // GROUPS)
    count = height * across * (width // GROUPS)
    center = lax.optimization_barrier(jnp.sum(grouped, axis=(0, 2))) / count
    offsets = grouped - center[None, :, None]
    spread = lax.optimization_barrier(jnp.sum(offsets * offsets, axis=(0, 2))) / count
    inverse = lax.rsqrt(spread + epsilon)
    return ((offsets * inverse[None, :, None]).reshape(values.shape), inverse)

def time_features(timestep):
    halfway = TFEAT // 2
    frequency = jnp.exp(-math.log(10000.0) * jnp.arange(halfway, dtype=jnp.float32) / halfway)
    angles = timestep.astype(jnp.float32)[:, None] * frequency[None, :]
    return jnp.concatenate([jnp.cos(angles), jnp.sin(angles)], axis=1)

def modulation(timestep, w_time, w_emb):
    embedded = jnp.dot(time_features(timestep), w_time.astype(jnp.float32), precision=lax.Precision.HIGHEST)
    return jnp.dot(jax.nn.silu(embedded), w_emb.astype(jnp.float32), precision=lax.Precision.HIGHEST)

def reference(features, timestep, w_time, w_emb, w_qkv, w_out, w_conv, upstream):
    shifts_all = modulation(timestep, w_time, w_emb)
    scales = shifts_all[:, :C]
    shifts = shifts_all[:, C:]
    cells = SIDE * SIDE

    def one_image(carry, item):
        image, cotangent, scale_row, shift_row = item
        normed, unused = normalize(image.astype(jnp.float32))
        tokens = normed.astype(jnp.bfloat16).reshape(cells, C)
        projected = jnp.dot(tokens, w_qkv, preferred_element_type=jnp.float32).astype(jnp.bfloat16)
        heads = projected.reshape(cells, 3, HEADS, HEAD_DIM).transpose(1, 2, 0, 3)

        def attend(triple):
            query, keys, values = triple
            scores = jnp.dot(query, keys.T, preferred_element_type=jnp.float32) / math.sqrt(HEAD_DIM)
            largest = lax.optimization_barrier(jnp.max(scores, axis=1, keepdims=True))
            weights = jnp.exp(scores - largest)
            total = lax.optimization_barrier(jnp.sum(weights, axis=1, keepdims=True))
            return jnp.dot(weights.astype(jnp.bfloat16), values, preferred_element_type=jnp.float32) / total
        mixed = lax.map(attend, (heads[0], heads[1], heads[2]))
        attended = mixed.transpose(1, 0, 2).reshape(cells, C).astype(jnp.bfloat16)
        hidden = (image.astype(jnp.float32).reshape(cells, C) + jnp.dot(attended, w_out, preferred_element_type=jnp.float32)).astype(jnp.bfloat16)
        hat, inverse = normalize(hidden.reshape(SIDE, SIDE, C).astype(jnp.float32))
        shifted = hat * (1.0 + scale_row) + shift_row
        activated = jax.nn.silu(shifted).astype(jnp.bfloat16)
        padded = jnp.pad(activated, ((1, 1), (1, 1), (0, 0)))
        padded_grad = jnp.pad(cotangent, ((1, 1), (1, 1), (0, 0)))
        flat_grad = cotangent.reshape(cells, C)
        result = jnp.zeros((cells, C), jnp.float32)
        back = jnp.zeros((cells, C), jnp.float32)
        pieces = []
        for position in range(9):
            row_step = position // 3
            col_step = position % 3
            window = padded[row_step:row_step + SIDE, col_step:col_step + SIDE].reshape(cells, C)
            kernel = w_conv[position * C:(position + 1) * C]
            result = result + jnp.dot(window, kernel, preferred_element_type=jnp.float32)
            pieces.append(jnp.dot(window.T, flat_grad, preferred_element_type=jnp.float32))
            moved = padded_grad[2 - row_step:2 - row_step + SIDE, 2 - col_step:2 - col_step + SIDE].reshape(cells, C)
            back = back + jnp.dot(moved, kernel.T, preferred_element_type=jnp.float32)
        back = back.reshape(SIDE, SIDE, C)
        sigma = jax.nn.sigmoid(shifted)
        through = back * sigma * (1.0 + shifted * (1.0 - sigma)) * (1.0 + scale_row)
        through_groups = through.reshape(cells, GROUPS, C // GROUPS)
        hat_groups = hat.reshape(cells, GROUPS, C // GROUPS)
        count = cells * (C // GROUPS)
        first_mean = lax.optimization_barrier(jnp.sum(through_groups, axis=(0, 2))) / count
        second_mean = lax.optimization_barrier(jnp.sum(through_groups * hat_groups, axis=(0, 2))) / count
        grad_hidden = inverse[None, :, None] * (through_groups - first_mean[None, :, None] - hat_groups * second_mean[None, :, None])
        grad_hidden = grad_hidden.reshape(SIDE, SIDE, C).astype(jnp.bfloat16)
        out_piece = jnp.dot(attended.T, grad_hidden.reshape(cells, C), preferred_element_type=jnp.float32)
        conv_total, out_total = carry
        conv_total = conv_total + jnp.concatenate(pieces, axis=0).reshape(-1)
        out_total = out_total + out_piece.reshape(-1)
        return ((conv_total, out_total), (result.reshape(SIDE, SIDE, C).astype(jnp.bfloat16), grad_hidden))
    initial = (jnp.zeros((9 * C * C,), jnp.float32), jnp.zeros((C * C,), jnp.float32))
    totals, outs_stacked = lax.scan(one_image, initial, (features, upstream, scales, shifts))
    return (outs_stacked[0], outs_stacked[1], totals[0], totals[1])
```

```python
import functools
import math

import jax
import jax.numpy as jnp
from jax import lax
from jax.experimental import pallas as pl
from jax.experimental.pallas import tpu as pltpu
from jax.sharding import PartitionSpec as P

MESH = pl.DeviceIdType.MESH
F32 = jnp.float32
BF16 = jnp.bfloat16
EPS = 1e-05
LOG2E = 1.4426950408889634
TFEAT = 128
N = 16
CELLS = 256
W = 512
NEAR = (0, 1, 7, 2, 6, 3, 5, 4)
FAR = (4, 3, 5, 2, 6, 1, 7)


def rcopy(src, dst, ssem, rsem, dev):
    return pltpu.make_async_remote_copy(
        src_ref=src, dst_ref=dst, send_sem=ssem, recv_sem=rsem, device_id=dev, device_id_type=MESH
    )


def loop(lo, hi, fn):
    def body(k, carry):
        fn(k)
        return carry

    lax.fori_loop(lo, hi, body, 0)


def share_start(buf, ssem, rsem, s):
    def go(k):
        t = lax.rem(s + k, N)
        rcopy(buf.at[s], buf.at[s], ssem.at[k], rsem.at[s], {"space": t}).start()

    loop(1, N, go)


def share_wait(buf, ssem, rsem, s):
    def go(k):
        t = lax.rem(s + k, N)
        copy = rcopy(buf.at[t], buf.at[t], ssem.at[k], rsem.at[t], {"space": t})
        copy.wait_send()
        copy.wait_recv()

    loop(1, N, go)


def group_sum(v):
    lane = lax.broadcasted_iota(jnp.int32, v.shape, 1)
    for k in (1, 2, 4, 8):
        v = v + jnp.where((lane & k) == 0, pltpu.roll(v, 128 - k, 1), pltpu.roll(v, k, 1))
    return v


def pack(a, b):
    return jnp.concatenate(
        [a[:, 128 * q : 128 * q + 128] for q in range(4)]
        + [b[:, 128 * q : 128 * q + 128] for q in range(4)],
        axis=0,
    )


def unpack(v, first=0):
    return jnp.concatenate([v[first + q : first + q + 1, :] for q in range(4)], axis=1)


def local_moments(values):
    mu = jnp.sum(values, axis=0, keepdims=True) / CELLS
    off = values - mu
    return pack(mu, jnp.sum(off * off, axis=0, keepdims=True))


def moments(buf):
    every = buf[...]
    total = jnp.sum(every, axis=0)
    mean = group_sum(total) / 256.0
    off = every - mean[None]
    spread = jnp.sum(off * off, axis=0) * CELLS + pltpu.roll(total, 4, 0)
    inverse = lax.rsqrt(group_sum(spread) / 65536.0 + EPS)
    return unpack(mean), unpack(inverse)


def dot(a, b):
    return jnp.dot(a, b, preferred_element_type=F32)


def dot_nt(a, b):
    return lax.dot_general(a, b, (((1,), (1,)), ((), ())), preferred_element_type=F32)


def exact_dot(v, w):
    high = v.astype(BF16)
    rest = v - high.astype(F32)
    mid = rest.astype(BF16)
    low = (rest - mid.astype(F32)).astype(BF16)
    return dot(high, w) + dot(mid, w) + dot(low, w)


def windows(v, dst):
    col = lax.broadcasted_iota(jnp.int32, v.shape, 0) & 63
    height = v.shape[0]
    dst[:, 0:W] = jnp.where(col != 0, pltpu.roll(v, 1, 0), 0.0).astype(BF16)
    dst[:, W : 2 * W] = v.astype(BF16)
    dst[:, 2 * W : 3 * W] = jnp.where(col != 63, pltpu.roll(v, height - 1, 0), 0.0).astype(BF16)


def silu(v):
    return v * jax.nn.sigmoid(v)


def kernel(
    x_ref, tf_ref, up_hbm, wtime_hbm, wemb_hbm, wqkv_hbm, wout_hbm, wconv_hbm,
    out_ref, gf_ref, gc_ref, go_ref,
    wtime, wemb, wqkv, wout, wconv,
    st1, st2, st3,
    kvs, qs, kvr, qr, val, score, prob, ats, atr, att,
    upp, pupp, umat, pumat, actp, amat, pact, patt, pgf, actt, attt,
    hat, zed, back, thr, mod,
    gst, grecv, gost, gorecv, sum2, piece32, piece, precv, opiece, oprecv,
    lsem,
    st_ssem, st_rsem,
    kv_ssem, kv_rsem, fw_ssem, q_ssem, q_rsem, at_ssem, at_rsem,
    halo_ssem, halo_rsem, pair_ssem, pair_rsem,
    g_ssem, g_rsem, o_ssem, o_rsem, p_ssem, p_rsem, op_ssem, op_rsem,
):
    d = lax.axis_index("dp")
    s = lax.axis_index("space")
    z = s // 2
    xl = lax.rem(s, 2)
    chip = d // 2
    core = lax.rem(d, 2)
    mate = {"dp": 2 * chip + 1 - core, "space": s}

    loads = [
        pltpu.make_async_copy(a, b, lsem.at[i])
        for i, (a, b) in enumerate(
            (
                (wqkv_hbm, wqkv),
                (up_hbm, upp.at[pl.ds(64, CELLS)]),
                (wtime_hbm, wtime),
                (wemb_hbm, wemb),
                (wconv_hbm, wconv),
                (wout_hbm, wout),
            )
        )
    ]
    for load in loads:
        load.start()

    blank = jnp.zeros((64, W), BF16)
    for ref in (upp, actp):
        ref[0:64, :] = blank
        ref[320:384, :] = blank

    barrier = pltpu.get_barrier_semaphore()

    def greet_space(k):
        pl.semaphore_signal(
            barrier, inc=1, device_id={"space": lax.rem(s + k, N)}, device_id_type=MESH
        )

    def greet_other_core(k):
        pl.semaphore_signal(
            barrier, inc=1, device_id={"dp": 2 * chip + 1 - core}, device_id_type=MESH
        )

    def greet_chips(k):
        pl.semaphore_signal(
            barrier,
            inc=1,
            device_id={"dp": 2 * lax.rem(chip + k, 8) + core},
            device_id_type=MESH,
        )

    loop(1, N, greet_space)
    loop(0, 1, greet_other_core)
    loop(1, 8, greet_chips)

    st1[s] = local_moments(x_ref[...].astype(F32))
    pl.semaphore_wait(barrier, 15 + 1 + 7)
    share_start(st1, st_ssem.at[0], st_rsem.at[0], s)

    loads[1].wait()
    up_top = rcopy(
        upp.at[pl.ds(64, 64)], upp.at[pl.ds(320, 64)], halo_ssem.at[0], halo_rsem.at[0],
        {"space": jnp.maximum(s - 1, 0)},
    )
    up_bottom = rcopy(
        upp.at[pl.ds(256, 64)], upp.at[pl.ds(0, 64)], halo_ssem.at[1], halo_rsem.at[1],
        {"space": jnp.minimum(s + 1, N - 1)},
    )

    @pl.when(s > 0)
    def _():
        up_top.start()

    @pl.when(s < N - 1)
    def _():
        up_bottom.start()

    share_wait(st1, st_ssem.at[0], st_rsem.at[0], s)
    mean1, inverse1 = moments(st1)
    normed = ((x_ref[...].astype(F32) - mean1) * inverse1).astype(BF16)
    loads[0].wait()
    low_half = lax.broadcasted_iota(jnp.int32, (CELLS, 128), 1) < 64
    low_short = lax.broadcasted_iota(jnp.int32, (128, 128), 1) < 64
    for pair in range(4):
        cols = [dot(normed, wqkv[:, W * j + 128 * pair : W * j + 128 * pair + 128]) for j in range(3)]
        q, k, v = cols
        q = q.astype(BF16).astype(F32) * 0.125
        turned_q = pltpu.roll(q, 64, 1)
        qs[2 * pair] = jnp.where(low_short, q[0:128], turned_q[128:256]).astype(BF16)
        qs[2 * pair + 1] = jnp.where(low_short, turned_q[0:128], q[128:256]).astype(BF16)
        kvs[2 * pair] = jnp.where(low_half, k, pltpu.roll(v, 64, 1)).astype(BF16)
        kvs[2 * pair + 1] = jnp.where(low_half, pltpu.roll(k, 64, 1), v).astype(BF16)

    for k in FAR:
        h = lax.rem(z + k, 8)
        dev = {"space": 2 * h + xl}
        rcopy(kvs.at[h], kvr.at[s], kv_ssem.at[k], kv_rsem.at[s], dev).start()
        rcopy(qs.at[h], qr.at[z], q_ssem.at[k], q_rsem.at[z], dev).start()
    kvr[s] = kvs[z]
    qr[z] = qs[z]

    loads[2].wait()
    loads[3].wait()
    embedded = exact_dot(tf_ref[...], wtime[...])
    mod[...] = exact_dot(silu(embedded), wemb[...])

    @pl.when(s < N - 1)
    def _():
        up_top.wait_recv()

    @pl.when(s > 0)
    def _():
        up_bottom.wait_recv()

    pair_up = rcopy(upp, pupp, pair_ssem.at[0], pair_rsem.at[0], mate)
    pair_up.start()
    windows(upp[...].astype(F32), umat)
    loads[4].wait()
    loads[5].wait()
    back[...] = jnp.zeros_like(back)

    def back_step(p):
        a = p // 3
        b = lax.rem(p, 3)
        rows = pl.ds(pl.multiple_of(64 * (2 - a), 64), CELLS)
        lanes = pl.ds(pl.multiple_of(W * (2 - b), W), W)
        back[...] += dot_nt(umat[rows, lanes], wconv[pl.ds(pl.multiple_of(W * p, W), W), :])

    loop(0, 9, back_step)
    pair_up.wait_recv()
    windows(pupp[...].astype(F32), pumat)

    other = {"space": 2 * z + 1 - xl}
    for k in NEAR:
        zz = lax.rem(z + k, 8)
        mine = 2 * zz + xl
        if k:
            rcopy(kvs.at[zz], kvr.at[mine], kv_ssem.at[k], kv_rsem.at[mine], other).wait_recv()
        rcopy(kvr.at[mine], kvr.at[mine], fw_ssem.at[k], kv_rsem.at[mine], other).start()
    for k in NEAR:
        zz = lax.rem(z + k, 8)
        if k:
            rcopy(qs.at[zz], qr.at[zz], q_ssem.at[k], q_rsem.at[zz], other).wait_recv()
    for k in NEAR:
        theirs = 2 * lax.rem(z + k, 8) + 1 - xl
        rcopy(kvr.at[theirs], kvr.at[theirs], fw_ssem.at[k], kv_rsem.at[theirs], other).wait_recv()

    def make_values(j):
        val[pl.ds(pl.multiple_of(CELLS * j, CELLS), CELLS), :] = jnp.where(
            low_half, 1.0, kvr[j].astype(F32)
        ).astype(BF16)

    loop(0, N, make_values)

    def attend(zz):
        q = qr[zz].astype(F32)
        qq = jnp.concatenate(
            [jnp.where(low_short, q, 0.0), jnp.where(low_short, pltpu.roll(q, 64, 1), 0.0)], axis=0
        ).astype(BF16)
        top = jnp.full((CELLS, 128), -jnp.inf, F32)
        for j in range(N):
            part = dot_nt(qq, kvr[j])
            score[:, CELLS * j : CELLS * j + CELLS] = part
            top = jnp.maximum(top, jnp.maximum(part[:, 0:128], part[:, 128:256]))
        top = jnp.max(top, axis=1, keepdims=True) * LOG2E
        for j in range(N):
            at = slice(CELLS * j, CELLS * j + CELLS)
            prob[:, at] = jnp.exp2(score[:, at] * LOG2E - top).astype(BF16)
        mixed = dot(prob[...], val[...])
        ratio = mixed / pltpu.roll(mixed, 64, 1)
        return jnp.where(low_short, pltpu.roll(ratio[0:128], 64, 1), ratio[128:256]).astype(BF16)

    def attend_far(k):
        zz = lax.rem(z + k, 8)
        ats[zz] = attend(zz)
        rcopy(
            ats.at[zz], atr.at[z], at_ssem.at[k], at_rsem.at[z], {"space": 2 * zz + xl}
        ).start()

    loop(1, 8, attend_far)
    atr[z] = attend(z)

    for k in NEAR[1:]:
        h = lax.rem(z + k, 8)
        rcopy(ats.at[h], atr.at[h], at_ssem.at[k], at_rsem.at[h], other).wait_recv()
    for pair in range(4):
        first = atr[2 * pair].astype(F32)
        second = atr[2 * pair + 1].astype(F32)
        lanes = slice(128 * pair, 128 * pair + 128)
        att[0:128, lanes] = jnp.where(low_short, first, pltpu.roll(second, 64, 1)).astype(BF16)
        att[128:256, lanes] = jnp.where(low_short, pltpu.roll(first, 64, 1), second).astype(BF16)
    pair_att = rcopy(att, patt, pair_ssem.at[1], pair_rsem.at[1], mate)
    pair_att.start()

    hidden = (x_ref[...].astype(F32) + dot(att[...], wout[...])).astype(BF16).astype(F32)
    st2[s] = local_moments(hidden)
    share_start(st2, st_ssem.at[1], st_rsem.at[1], s)
    thr[...] = hidden
    share_wait(st2, st_ssem.at[1], st_rsem.at[1], s)
    mean2, inverse2 = moments(st2)
    scale = 1.0 + mod[0:1, 0:W]
    shift = mod[0:1, W : 2 * W]
    hats = (thr[...] - mean2) * inverse2
    hat[...] = hats
    shifted = hats * scale + shift
    zed[...] = shifted
    actp[64:320, :] = silu(shifted).astype(BF16)

    act_top = rcopy(
        actp.at[pl.ds(64, 64)], actp.at[pl.ds(320, 64)], halo_ssem.at[2], halo_rsem.at[2],
        {"space": jnp.maximum(s - 1, 0)},
    )
    act_bottom = rcopy(
        actp.at[pl.ds(256, 64)], actp.at[pl.ds(0, 64)], halo_ssem.at[3], halo_rsem.at[3],
        {"space": jnp.minimum(s + 1, N - 1)},
    )

    @pl.when(s > 0)
    def _():
        act_top.start()

    @pl.when(s < N - 1)
    def _():
        act_bottom.start()

    pair_act = rcopy(actp.at[pl.ds(64, CELLS)], pact, pair_ssem.at[2], pair_rsem.at[2], mate)
    pair_act.start()

    sigma = jax.nn.sigmoid(zed[...])
    through = back[...] * sigma * (1.0 + zed[...] * (1.0 - sigma)) * scale
    thr[...] = through
    st3[s] = pack(
        jnp.sum(through, axis=0, keepdims=True),
        jnp.sum(through * hat[...], axis=0, keepdims=True),
    )
    share_start(st3, st_ssem.at[2], st_rsem.at[2], s)

    actt[:, 0:CELLS] = actp[64:320, :].T
    pair_act.wait_recv()
    actt[:, CELLS : 2 * CELLS] = pact[...].T

    def grad_step(j):
        p = lax.rem(chip + 1 + j, 9)
        a = p // 3
        b = lax.rem(p, 3)
        rows = pl.ds(pl.multiple_of(64 * (2 - a), 64), CELLS)
        lanes = pl.ds(pl.multiple_of(W * (2 - b), W), W)
        part = dot(actt[:, 0:CELLS], umat[rows, lanes]) + dot(
            actt[:, CELLS : 2 * CELLS], pumat[rows, lanes]
        )
        gst[pl.ds(pl.multiple_of(W * p, W), W), :] = part.astype(BF16)

        @pl.when((j >= 1) & (p >= 1))
        def _():
            to = p - 1
            rcopy(
                gst.at[pl.ds(pl.multiple_of(576 * to + 288 * core, 32), 288)],
                grecv.at[chip],
                g_ssem.at[to],
                g_rsem.at[chip],
                {"dp": 2 * to + core},
            ).start()

    loop(0, 9, grad_step)

    share_wait(st3, st_ssem.at[2], st_rsem.at[2], s)
    sums = group_sum(jnp.sum(st3[...], axis=0)) / 65536.0
    gf = (inverse2 * (thr[...] - unpack(sums) - hat[...] * unpack(sums, 4))).astype(BF16)
    gf_ref[...] = gf
    pair_gf = rcopy(gf_ref, pgf, pair_ssem.at[3], pair_rsem.at[3], mate)
    pair_gf.start()
    pair_att.wait_recv()
    attt[:, 0:CELLS] = att[...].T
    attt[:, CELLS : 2 * CELLS] = patt[...].T
    pair_gf.wait_recv()
    gost[...] = (
        dot(attt[:, 0:CELLS], gf_ref[...]) + dot(attt[:, CELLS : 2 * CELLS], pgf[...])
    ).astype(BF16)

    def send_out(k):
        to = lax.rem(chip + k, 8)
        rcopy(
            gost.at[pl.ds(pl.multiple_of(64 * to + 32 * core, 32), 32)],
            gorecv.at[chip],
            o_ssem.at[to],
            o_rsem.at[chip],
            {"dp": 2 * to + core},
        ).start()

    loop(1, 8, send_out)

    @pl.when(s < N - 1)
    def _():
        act_top.wait_recv()

    @pl.when(s > 0)
    def _():
        act_bottom.wait_recv()

    windows(actp[...].astype(F32), amat)
    thr[...] = jnp.zeros_like(thr)

    def conv_step(a):
        thr[...] += dot(
            amat[pl.ds(pl.multiple_of(64 * a, 64), CELLS), :],
            wconv[pl.ds(pl.multiple_of(3 * W * a, W), 3 * W), :],
        )

    loop(0, 3, conv_step)
    out_ref[...] = thr[...].astype(BF16)

    def take_out(k):
        frm = lax.rem(chip + k, 8)
        rcopy(gorecv.at[frm], gorecv.at[frm], o_ssem.at[frm], o_rsem.at[frm], mate).wait_recv()

    loop(1, 8, take_out)
    gorecv[chip] = gost[pl.ds(pl.multiple_of(64 * chip + 32 * core, 32), 32), :]
    out_sum = jnp.sum(gorecv[...].astype(F32), axis=0)
    for t in range(N):
        rows = out_sum[2 * t : 2 * t + 2]
        opiece[t] = pack(rows[0:1], rows[1:2])

    def send_opiece(k):
        t = lax.rem(s + k, N)
        rcopy(opiece.at[t], oprecv.at[s], op_ssem.at[k], op_rsem.at[s], {"space": t}).start()

    loop(1, N, send_opiece)
    oprecv[s] = opiece[s]

    def take_grad(k):
        frm = lax.rem(chip + k, 8)
        rcopy(grecv.at[frm], grecv.at[frm], g_ssem.at[frm], g_rsem.at[frm], mate).wait_recv()

    loop(1, 8, take_grad)
    grecv[chip] = gst[pl.ds(pl.multiple_of(576 * chip + 288 * core, 32), 288), :]
    sum2[...] = jnp.zeros_like(sum2)

    def add_grad(k):
        sum2[...] += grecv[k].astype(F32)

    loop(0, 8, add_grad)
    for t in range(N):
        for q in range(4):
            piece32[18 * q : 18 * q + 18, :] = sum2[18 * t : 18 * t + 18, 128 * q : 128 * q + 128]
        piece32[72:80, :] = jnp.zeros((8, 128), F32)
        piece[t] = piece32[...].astype(BF16)

    def send_piece(k):
        t = lax.rem(s + k, N)
        rcopy(piece.at[t], precv.at[s], p_ssem.at[k], p_rsem.at[s], {"space": t}).start()

    loop(1, N, send_piece)
    precv[s] = piece[s]

    def take_pieces(k):
        t = lax.rem(s + k, N)
        o = rcopy(opiece.at[t], oprecv.at[t], op_ssem.at[k], op_rsem.at[t], {"space": t})
        o.wait_send()
        o.wait_recv()
        g = rcopy(piece.at[t], precv.at[t], p_ssem.at[k], p_rsem.at[t], {"space": t})
        g.wait_send()
        g.wait_recv()

    loop(1, N, take_pieces)
    owned_out = jnp.sum(oprecv[...], axis=0)
    go_ref[...] = jnp.concatenate([unpack(owned_out), unpack(owned_out, 4)], axis=0)
    piece32[...] = jnp.sum(precv[...].astype(F32), axis=0)
    for q in range(4):
        gc_ref[:, 128 * q : 128 * q + 128] = piece32[18 * q : 18 * q + 18, :]

    for k in range(8):
        zz = lax.rem(z + k, 8)
        rcopy(kvr.at[0], kvr.at[0], fw_ssem.at[k], kv_rsem.at[0], other).wait_send()
        if k:
            rcopy(kvs.at[zz], kvr.at[0], kv_ssem.at[k], kv_rsem.at[0], other).wait_send()
            rcopy(qs.at[zz], qr.at[0], q_ssem.at[k], q_rsem.at[0], other).wait_send()
            rcopy(ats.at[zz], atr.at[0], at_ssem.at[k], at_rsem.at[0], other).wait_send()

    def chips_sent(k):
        to = lax.rem(chip + k, 8)
        rcopy(gorecv.at[to], gorecv.at[to], o_ssem.at[to], o_rsem.at[to], mate).wait_send()
        rcopy(grecv.at[to], grecv.at[to], g_ssem.at[to], g_rsem.at[to], mate).wait_send()

    loop(1, 8, chips_sent)
    for copy in (pair_up, pair_att, pair_act, pair_gf):
        copy.wait_send()

    @pl.when(s > 0)
    def _():
        up_top.wait_send()
        act_top.wait_send()

    @pl.when(s < N - 1)
    def _():
        up_bottom.wait_send()
        act_bottom.wait_send()


def time_features(timestep):
    halfway = TFEAT // 2
    frequency = jnp.exp(-math.log(10000.0) * jnp.arange(halfway, dtype=F32) / halfway)
    angles = timestep.astype(F32)[:, None] * frequency[None, :]
    return jnp.concatenate([jnp.cos(angles), jnp.sin(angles)], axis=1)


def on_device(features, timestep, w_time, w_emb, w_qkv, w_out, w_conv, upstream):
    tfeat = jnp.broadcast_to(time_features(timestep), (8, TFEAT))
    vmem = pl.BlockSpec(memory_space=pltpu.VMEM)
    hbm = pl.BlockSpec(memory_space=pl.ANY)
    V = pltpu.VMEM
    dma = pltpu.SemaphoreType.DMA
    scratch = [
        V((TFEAT, W), BF16), V((W, 2 * W), BF16), V((W, 3 * W), BF16), V((W, W), BF16), V((9 * W, W), BF16),
        V((N, 8, 128), F32), V((N, 8, 128), F32), V((N, 8, 128), F32),
        V((8, CELLS, 128), BF16), V((8, 128, 128), BF16), V((N, CELLS, 128), BF16), V((8, 128, 128), BF16),
        V((N * CELLS, 128), BF16), V((CELLS, N * CELLS), F32), V((CELLS, N * CELLS), BF16),
        V((8, 128, 128), BF16), V((8, 128, 128), BF16), V((CELLS, W), BF16),
        V((384, W), BF16), V((384, W), BF16), V((384, 3 * W), BF16), V((384, 3 * W), BF16),
        V((384, W), BF16), V((384, 3 * W), BF16),
        V((CELLS, W), BF16), V((CELLS, W), BF16), V((CELLS, W), BF16),
        V((W, 2 * CELLS), BF16), V((W, 2 * CELLS), BF16),
        V((CELLS, W), F32), V((CELLS, W), F32), V((CELLS, W), F32), V((CELLS, W), F32), V((8, 2 * W), F32),
        V((9 * W, W), BF16), V((8, 288, W), BF16), V((W, W), BF16), V((8, 32, W), BF16),
        V((288, W), F32), V((80, 128), F32), V((N, 80, 128), BF16), V((N, 80, 128), BF16),
        V((N, 8, 128), F32), V((N, 8, 128), F32),
        dma((6,)),
        dma((3, N)), dma((3, N)),
        dma((8,)), dma((N,)), dma((8,)), dma((8,)), dma((8,)), dma((8,)), dma((8,)),
        dma((4,)), dma((4,)), dma((4,)), dma((4,)),
        dma((8,)), dma((8,)), dma((8,)), dma((8,)), dma((N,)), dma((N,)), dma((N,)), dma((N,)),
    ]
    out, gf, gc, go = pl.pallas_call(
        kernel,
        out_shape=(
            jax.ShapeDtypeStruct((CELLS, W), BF16),
            jax.ShapeDtypeStruct((CELLS, W), BF16),
            jax.ShapeDtypeStruct((18, W), F32),
            jax.ShapeDtypeStruct((2, W), F32),
        ),
        in_specs=[vmem, vmem, hbm, hbm, hbm, hbm, hbm, hbm],
        out_specs=(vmem, vmem, vmem, vmem),
        scratch_shapes=scratch,
        compiler_params=pltpu.CompilerParams(
            collective_id=0, has_side_effects=True, vmem_limit_bytes=60 * 1024 * 1024
        ),
    )(
        features.reshape(CELLS, W), tfeat, upstream.reshape(CELLS, W),
        w_time, w_emb, w_qkv, w_out, w_conv,
    )
    return (
        out.reshape(features.shape),
        gf.reshape(features.shape),
        gc.reshape(-1),
        go.reshape(-1),
    )


def solution(mesh):
    return jax.shard_map(
        on_device,
        mesh=mesh,
        in_specs=(
            P("dp", "space", None, None), P("dp"), P(), P(), P(), P(), P(),
            P("dp", "space", None, None),
        ),
        out_specs=(
            P("dp", "space", None, None), P("dp", "space", None, None),
            P(("dp", "space")), P(("dp", "space")),
        ),
        check_vma=False,
    )
```

```python
import functools
import math

import jax
import jax.numpy as jnp
from jax import lax
from jax.experimental import pallas as pl
from jax.experimental.pallas import tpu as pltpu
from jax.sharding import PartitionSpec as P

MESH = pl.DeviceIdType.MESH
F32 = jnp.float32
BF16 = jnp.bfloat16
EPS = 1e-05
LOG2E = 1.4426950408889634
TFEAT = 128
N = 16
CELLS = 256
W = 512
HALF = 256
NEAR = (0, 1, 7, 2, 6, 3, 5, 4)


def rcopy(src, dst, ssem, rsem, dev):
    return pltpu.make_async_remote_copy(
        src_ref=src, dst_ref=dst, send_sem=ssem, recv_sem=rsem, device_id=dev, device_id_type=MESH
    )


def loop(lo, hi, fn):
    def body(k, carry):
        fn(k)
        return carry

    lax.fori_loop(lo, hi, body, 0)


def share_start(buf, ssem, rsem, s):
    def go(k):
        t = lax.rem(s + k, N)
        rcopy(buf.at[s], buf.at[s], ssem.at[k], rsem.at[s], {"space": t}).start()

    loop(1, N, go)


def share_wait(buf, ssem, rsem, s):
    def go(k):
        t = lax.rem(s + k, N)
        copy = rcopy(buf.at[t], buf.at[t], ssem.at[k], rsem.at[t], {"space": t})
        copy.wait_send()
        copy.wait_recv()

    loop(1, N, go)


def group_sum(v):
    lane = lax.broadcasted_iota(jnp.int32, v.shape, 1)
    for k in (1, 2, 4, 8):
        v = v + jnp.where((lane & k) == 0, pltpu.roll(v, 128 - k, 1), pltpu.roll(v, k, 1))
    return v


def pack(a, b):
    return jnp.concatenate(
        [a[:, 128 * q : 128 * q + 128] for q in range(4)]
        + [b[:, 128 * q : 128 * q + 128] for q in range(4)],
        axis=0,
    )


def unpack(v, first=0):
    return jnp.concatenate([v[first + q : first + q + 1, :] for q in range(4)], axis=1)


def local_moments(values):
    mu = jnp.sum(values, axis=0, keepdims=True) / CELLS
    off = values - mu
    return pack(mu, jnp.sum(off * off, axis=0, keepdims=True))


def moments(buf):
    every = buf[...]
    total = jnp.sum(every, axis=0)
    mean = group_sum(total) / 256.0
    off = every - mean[None]
    spread = jnp.sum(off * off, axis=0) * CELLS + pltpu.roll(total, 4, 0)
    inverse = lax.rsqrt(group_sum(spread) / 65536.0 + EPS)
    return unpack(mean), unpack(inverse)


def dot(a, b):
    return jnp.dot(a, b, preferred_element_type=F32)


def dot_nt(a, b):
    return lax.dot_general(a, b, (((1,), (1,)), ((), ())), preferred_element_type=F32)


def exact_dot(v, w):
    high = v.astype(BF16)
    rest = v - high.astype(F32)
    mid = rest.astype(BF16)
    low = (rest - mid.astype(F32)).astype(BF16)
    return dot(high, w) + dot(mid, w) + dot(low, w)


def windows(v, dst):
    col = lax.broadcasted_iota(jnp.int32, v.shape, 0) & 63
    height, width = v.shape
    dst[:, 0:width] = jnp.where(col != 0, pltpu.roll(v, 1, 0), 0.0).astype(BF16)
    dst[:, width : 2 * width] = v.astype(BF16)
    dst[:, 2 * width : 3 * width] = jnp.where(col != 63, pltpu.roll(v, height - 1, 0), 0.0).astype(
        BF16
    )


def silu(v):
    return v * jax.nn.sigmoid(v)


def kernel(
    x_hbm, tf_ref, up_hbm, wtime_hbm, wemb_hbm, wqkv_hbm, wout_hbm, wconv_hbm,
    out_hbm, gf_hbm, gc_ref, go_ref,
    x_ref, wtime, wemb, wqkv, wout, wconv,
    st1, st2, st3,
    kvs, qs, kvr, qr, qq, val, top, acc, ats, atr, att,
    upp, uo, uh, umat, umat4,
    hid, hx, hfar, actp, xact, amat, patt, gf_ref, pgf, actt, attt,
    out_ref, hat, zed, back, thr, mod,
    gst, grecv, gost, gorecv, sum2, piece32, piece, precv, opiece, oprecv,
    lsem,
    st_ssem, st_rsem,
    kv_ssem, kv_rsem, fw_ssem, q_ssem, q_rsem, at_ssem, at_rsem,
    halo_ssem, halo_rsem, pair_ssem, pair_rsem,
    g_ssem, g_rsem, o_ssem, o_rsem, p_ssem, p_rsem, op_ssem, op_rsem,
):
    d = lax.axis_index("dp")
    s = lax.axis_index("space")
    z = s // 2
    xl = lax.rem(s, 2)
    chip = d // 2
    core = lax.rem(d, 2)
    mate = {"dp": 2 * chip + 1 - core}
    other = {"space": 2 * z + 1 - xl}

    barrier = pltpu.get_barrier_semaphore()

    def greet(dev):
        pl.semaphore_signal(barrier, inc=1, device_id=dev, device_id_type=MESH)

    loop(1, N, lambda k: greet({"space": lax.rem(s + k, N)}))
    loop(1, 8, lambda k: greet({"dp": 2 * lax.rem(chip + k, 8) + core}))
    greet(mate)

    loads = [
        pltpu.make_async_copy(a, b, lsem.at[i])
        for i, (a, b) in enumerate(
            (
                (x_hbm, x_ref),
                (wqkv_hbm, wqkv),
                (up_hbm, upp.at[pl.ds(64, CELLS)]),
                (wtime_hbm, wtime),
                (wemb_hbm, wemb),
                (wconv_hbm, wconv),
                (wout_hbm, wout),
            )
        )
    ]
    loads[0].start()
    loads[1].start()

    blank = jnp.zeros((64, W), BF16)

    @pl.when(s == 0)
    def _():
        upp[0:64, :] = blank

    @pl.when(s == N - 1)
    def _():
        upp[320:384, :] = blank

    loads[0].wait()
    st1[s] = local_moments(x_ref[...].astype(F32))
    for load in loads[2:]:
        load.start()
    pl.semaphore_wait(barrier, 15 + 7 + 1)
    share_start(st1, st_ssem.at[0], st_rsem.at[0], s)

    loads[2].wait()
    up_top = rcopy(
        upp.at[pl.ds(64, 64)], upp.at[pl.ds(320, 64)], halo_ssem.at[0], halo_rsem.at[0],
        {"space": jnp.maximum(s - 1, 0)},
    )
    up_bottom = rcopy(
        upp.at[pl.ds(256, 64)], upp.at[pl.ds(0, 64)], halo_ssem.at[1], halo_rsem.at[1],
        {"space": jnp.minimum(s + 1, N - 1)},
    )

    @pl.when(s > 0)
    def _():
        up_top.start()

    @pl.when(s < N - 1)
    def _():
        up_bottom.start()


    loads[1].wait()
    share_wait(st1, st_ssem.at[0], st_rsem.at[0], s)
    mean1, inverse1 = moments(st1)
    normed = ((x_ref[...].astype(F32) - mean1) * inverse1).astype(BF16)
    low_half = lax.broadcasted_iota(jnp.int32, (CELLS, 128), 1) < 64
    low_short = lax.broadcasted_iota(jnp.int32, (128, 128), 1) < 64
    for pair in range(4):
        q = dot(normed, wqkv[:, 128 * pair : 128 * pair + 128])
        q = q.astype(BF16).astype(F32) * 0.125
        turned = pltpu.roll(q, 64, 1)
        qs[2 * pair] = jnp.where(low_short, q[0:128], turned[128:256]).astype(BF16)
        qs[2 * pair + 1] = jnp.where(low_short, turned[0:128], q[128:256]).astype(BF16)

    def q_copy(p):
        h = lax.rem(z + NEAR[p], 8)
        slot = NEAR.index((8 - NEAR[p]) % 8)
        return rcopy(
            qs.at[h], qr.at[slot], q_ssem.at[p], q_rsem.at[slot], {"space": 2 * h + xl}
        )

    def kv_copy(p):
        h = lax.rem(z + NEAR[p], 8)
        slot = NEAR.index((8 - NEAR[p]) % 8)
        return rcopy(
            kvs.at[h], kvr.at[slot], kv_ssem.at[p], kv_rsem.at[slot], {"space": 2 * h + xl}
        )

    def forward(p):
        return rcopy(kvr.at[p], kvr.at[8 + p], fw_ssem.at[p], kv_rsem.at[8 + p], other)

    for p in range(1, 8):
        q_copy(p).start()
    for pair in range(4):
        k = dot(normed, wqkv[:, W + 128 * pair : W + 128 * pair + 128])
        v = dot(normed, wqkv[:, 2 * W + 128 * pair : 2 * W + 128 * pair + 128])
        kvs[2 * pair] = jnp.where(low_half, k, pltpu.roll(v, 64, 1)).astype(BF16)
        kvs[2 * pair + 1] = jnp.where(low_half, pltpu.roll(k, 64, 1), v).astype(BF16)
    for p in (1, 2):
        kv_copy(p).start()
    kvr[0] = kvs[z]
    qr[0] = qs[z]
    forward(0).start()

    loads[3].wait()
    loads[4].wait()
    embedded = exact_dot(tf_ref[...], wtime[...])
    mod[...] = exact_dot(silu(embedded), wemb[...])

    @pl.when(s < N - 1)
    def _():
        up_top.wait_recv()

    @pl.when(s > 0)
    def _():
        up_bottom.wait_recv()

    uh[0] = upp[:, pl.ds(pl.multiple_of(HALF * xl, HALF), HALF)]
    uo[...] = upp[:, pl.ds(pl.multiple_of(HALF * (1 - xl), HALF), HALF)]
    up_mate = rcopy(uh.at[0], uh.at[2], pair_ssem.at[0], pair_rsem.at[0], mate)
    up_other = rcopy(uo, uh.at[1], pair_ssem.at[1], pair_rsem.at[1], other)
    up_both = rcopy(uh.at[1], uh.at[3], pair_ssem.at[2], pair_rsem.at[2], mate)
    up_mate.start()
    up_other.start()
    windows(upp[...].astype(F32), umat)
    windows(uh[0].astype(F32), umat4.at[0])
    loads[5].wait()
    loads[6].wait()
    back[...] = jnp.zeros_like(back)

    def back_step(p):
        a = p // 3
        b = lax.rem(p, 3)
        rows = pl.ds(pl.multiple_of(64 * (2 - a), 64), CELLS)
        lanes = pl.ds(pl.multiple_of(W * (2 - b), W), W)
        back[...] += dot_nt(umat[rows, lanes], wconv[pl.ds(pl.multiple_of(W * p, W), W), :])

    loop(0, 9, back_step)

    for p in range(1, 8):
        q_copy(NEAR.index((8 - NEAR[p]) % 8)).wait_recv()
    kv_copy(3).start()
    kv_copy(4).start()
    for p in range(8):
        q = qr[p].astype(F32)
        qq[p, 0:128, :] = jnp.where(low_short, q, 0.0).astype(BF16)
        qq[p, 128:256, :] = jnp.where(low_short, pltpu.roll(q, 64, 1), 0.0).astype(BF16)

    def take(p):
        if 1 <= p < 8:
            kv_copy(NEAR.index((8 - NEAR[p]) % 8)).wait_recv()
            forward(p).start()
        if p >= 8:
            forward(p - 8).wait_recv()
        val[p] = jnp.where(low_half, 1.0, kvr[p].astype(F32)).astype(BF16)

    def attend(i, slots, first, last):
        query = qq[i]
        parts = [dot_nt(query, kvr[p]) for p in slots]
        high = None
        for part in parts:
            part = jnp.maximum(part[:, 0:128], part[:, 128:256])
            high = part if high is None else jnp.maximum(high, part)
        high = jnp.max(high, axis=1, keepdims=True) * LOG2E
        if not first:
            before = top[i]
            high = jnp.maximum(before, high)
        else:
            high = jnp.broadcast_to(high, (CELLS, 128))
        wide = jnp.concatenate([high, high], axis=1)
        total = None
        for part, p in zip(parts, slots):
            mixed = dot(jnp.exp2(part * LOG2E - wide).astype(BF16), val[p])
            total = mixed if total is None else total + mixed
        if not first:
            total = total + acc[i] * jnp.exp2(before - high)
        if last:
            return total
        top[i] = high
        acc[i] = total

    def finish(total):
        ratio = total / pltpu.roll(total, 64, 1)
        return jnp.where(low_short, pltpu.roll(ratio[0:128], 64, 1), ratio[128:256]).astype(BF16)

    def go(*slots):
        loop(0, 8, lambda i: attend(i, slots, 0 in slots, False))

    take(0)
    take(1)
    take(2)
    kv_copy(5).start()
    kv_copy(6).start()
    go(0, 1, 2)
    take(3)
    take(4)
    kv_copy(7).start()
    up_other.wait_recv()
    up_both.start()
    take(8)
    go(3, 4, 8)
    take(9)
    take(10)
    take(5)
    take(6)
    go(9, 10, 5, 6)
    take(7)
    take(11)
    take(12)
    go(7, 11, 12)
    for p in (13, 14, 15):
        take(p)

    def last_far(k):
        i = 8 - k
        zz = lax.rem(z + jnp.where(lax.rem(i, 2) == 1, (i + 1) // 2, 8 - i // 2), 8)
        ats[i] = finish(attend(i, (13, 14, 15), False, True))
        rcopy(
            ats.at[i], atr.at[z], at_ssem.at[i], at_rsem.at[z], {"space": 2 * zz + xl}
        ).start()

    loop(1, 8, last_far)
    atr[z] = finish(attend(0, (13, 14, 15), False, True))

    windows(uh[1].astype(F32), umat4.at[1])
    for k in range(1, 8):
        h = lax.rem(z + k, 8)
        rcopy(ats.at[k], atr.at[h], at_ssem.at[k], at_rsem.at[h], other).wait_recv()
    for pair in range(4):
        first = atr[2 * pair].astype(F32)
        second = atr[2 * pair + 1].astype(F32)
        lanes = slice(128 * pair, 128 * pair + 128)
        att[0:128, lanes] = jnp.where(low_short, first, pltpu.roll(second, 64, 1)).astype(BF16)
        att[128:256, lanes] = jnp.where(low_short, pltpu.roll(first, 64, 1), second).astype(BF16)

    hidden = (x_ref[...].astype(F32) + dot(att[...], wout[...])).astype(BF16)
    hid[...] = hidden
    hidden = hidden.astype(F32)
    st2[s] = local_moments(hidden)
    share_start(st2, st_ssem.at[1], st_rsem.at[1], s)
    far = s - 1 + 2 * xl
    has_far = (far >= 0) & (far < N)
    hid_far = rcopy(
        hid.at[pl.ds(pl.multiple_of(192 * xl, 64), 64)], hfar, halo_ssem.at[2], halo_rsem.at[2],
        {"space": jnp.clip(far, 0, N - 1)},
    )

    @pl.when(has_far)
    def _():
        hid_far.start()

    hid_other = rcopy(hid, hx, pair_ssem.at[3], pair_rsem.at[3], other)
    hid_other.start()
    pair_att = rcopy(att, patt, pair_ssem.at[4], pair_rsem.at[4], mate)
    pair_att.start()
    up_mate.wait_recv()
    windows(uh[2].astype(F32), umat4.at[2])
    up_both.wait_recv()
    windows(uh[3].astype(F32), umat4.at[3])
    attt[:, 0:CELLS] = att[...].T
    pair_att.wait_recv()
    attt[:, CELLS : 2 * CELLS] = patt[...].T

    share_wait(st2, st_ssem.at[1], st_rsem.at[1], s)
    mean2, inverse2 = moments(st2)
    scale = 1.0 + mod[0:1, 0:W]
    shift = mod[0:1, W : 2 * W]
    gain = inverse2 * scale

    def act_of(ref):
        return silu((ref[...].astype(F32) - mean2) * inverse2 * scale + shift).astype(BF16)

    hats = (hid[...].astype(F32) - mean2) * inverse2
    hat[...] = hats
    shifted = hats * scale + shift
    sigma = jax.nn.sigmoid(shifted)
    act = (shifted * sigma).astype(BF16)
    actp[64:320, :] = act
    actt[:, 0:CELLS] = act.T
    hid_other.wait_recv()
    xact[...] = act_of(hx)
    actt[:, CELLS : 2 * CELLS] = xact[...].T
    pair_act = rcopy(
        actt.at[:, pl.ds(0, 2 * CELLS)], actt.at[:, pl.ds(2 * CELLS, 2 * CELLS)],
        pair_ssem.at[5], pair_rsem.at[5], mate,
    )
    pair_act.start()

    through = back[...] * sigma * (1.0 + shifted * (1.0 - sigma)) * scale
    thr[...] = through
    st3[s] = pack(
        jnp.sum(through, axis=0, keepdims=True),
        jnp.sum(through * hats, axis=0, keepdims=True),
    )
    share_start(st3, st_ssem.at[2], st_rsem.at[2], s)

    actp[pl.ds(pl.multiple_of(320 * (1 - xl), 64), 64), :] = xact[
        pl.ds(pl.multiple_of(192 * xl, 64), 64), :
    ]
    edge = pl.ds(pl.multiple_of(320 * xl, 64), 64)

    @pl.when(has_far)
    def _():
        hid_far.wait_recv()
        actp[edge, :] = act_of(hfar)

    @pl.when(jnp.logical_not(has_far))
    def _():
        actp[edge, :] = blank

    windows(actp[...].astype(F32), amat)
    pair_act.wait_recv()

    def grad_step(j):
        p = lax.rem(chip + 1 + j, 9)
        a = p // 3
        b = lax.rem(p, 3)
        rows = pl.ds(pl.multiple_of(64 * (2 - a), 64), CELLS)
        lanes = pl.ds(pl.multiple_of(HALF * (2 - b), HALF), HALF)
        part = dot(actt[:, 0:CELLS], umat4[0, rows, lanes])
        for i in range(1, 4):
            part += dot(actt[:, CELLS * i : CELLS * i + CELLS], umat4[i, rows, lanes])
        gst[pl.ds(pl.multiple_of(W * p, W), W), :] = part.astype(BF16)

        @pl.when((j >= 1) & (p >= 1))
        def _():
            to = p - 1
            rcopy(
                gst.at[pl.ds(pl.multiple_of(576 * to + 288 * core, 32), 288)],
                grecv.at[chip],
                g_ssem.at[to],
                g_rsem.at[chip],
                {"dp": 2 * to + core},
            ).start()

    loop(0, 9, grad_step)

    share_wait(st3, st_ssem.at[2], st_rsem.at[2], s)
    sums = group_sum(jnp.sum(st3[...], axis=0)) / 65536.0
    gf_ref[...] = (inverse2 * (thr[...] - unpack(sums) - hat[...] * unpack(sums, 4))).astype(BF16)
    pair_gf = rcopy(gf_ref, pgf, pair_ssem.at[6], pair_rsem.at[6], mate)
    pair_gf.start()
    gf_out = pltpu.make_async_copy(gf_ref, gf_hbm, lsem.at[7])
    gf_out.start()
    part = dot(attt[:, 0:CELLS], gf_ref[...])
    pair_gf.wait_recv()
    gost[...] = (part + dot(attt[:, CELLS : 2 * CELLS], pgf[...])).astype(BF16)

    def send_out(k):
        to = lax.rem(chip + k, 8)
        rcopy(
            gost.at[pl.ds(pl.multiple_of(64 * to + 32 * core, 32), 32)],
            gorecv.at[chip],
            o_ssem.at[to],
            o_rsem.at[chip],
            {"dp": 2 * to + core},
        ).start()

    loop(1, 8, send_out)

    thr[...] = jnp.zeros_like(thr)

    def conv_step(a):
        thr[...] += dot(
            amat[pl.ds(pl.multiple_of(64 * a, 64), CELLS), :],
            wconv[pl.ds(pl.multiple_of(3 * W * a, W), 3 * W), :],
        )

    loop(0, 3, conv_step)
    out_ref[...] = thr[...].astype(BF16)
    out_out = pltpu.make_async_copy(out_ref, out_hbm, lsem.at[8])
    out_out.start()

    def take_grad(k):
        frm = lax.rem(chip + k, 8)
        rcopy(grecv.at[frm], grecv.at[frm], g_ssem.at[frm], g_rsem.at[frm], mate).wait_recv()

    loop(1, 8, take_grad)
    grecv[chip] = gst[pl.ds(pl.multiple_of(576 * chip + 288 * core, 32), 288), :]
    sum2[...] = jnp.sum(grecv[...].astype(F32), axis=0)
    piece32[...] = jnp.zeros_like(piece32)
    for t in range(N):
        for q in range(2):
            piece32[pl.ds(q, 18, stride=2), :] = sum2[18 * t : 18 * t + 18, 128 * q : 128 * q + 128]
        piece[t] = piece32[...].astype(BF16)

    def send_piece(k):
        t = lax.rem(s + k, N)
        rcopy(piece.at[t], precv.at[s], p_ssem.at[k], p_rsem.at[s], {"space": t}).start()

    loop(1, N, send_piece)
    precv[s] = piece[s]

    def take_out(k):
        frm = lax.rem(chip + k, 8)
        rcopy(gorecv.at[frm], gorecv.at[frm], o_ssem.at[frm], o_rsem.at[frm], mate).wait_recv()

    loop(1, 8, take_out)
    gorecv[chip] = gost[pl.ds(pl.multiple_of(64 * chip + 32 * core, 32), 32), :]
    out_sum = jnp.sum(gorecv[...].astype(F32), axis=0)
    for t in range(N):
        opiece[t] = pack(out_sum[2 * t : 2 * t + 1], out_sum[2 * t + 1 : 2 * t + 2])

    def send_opiece(k):
        t = lax.rem(s + k, N)
        rcopy(opiece.at[t], oprecv.at[s], op_ssem.at[k], op_rsem.at[s], {"space": t}).start()

    loop(1, N, send_opiece)
    oprecv[s] = opiece[s]

    for p in range(8):
        forward(p).wait_send()
        if p:
            kv_copy(p).wait_send()
            q_copy(p).wait_send()
            rcopy(ats.at[p], atr.at[0], at_ssem.at[p], at_rsem.at[0], other).wait_send()

    def chips_sent(k):
        to = lax.rem(chip + k, 8)
        rcopy(gorecv.at[to], gorecv.at[to], o_ssem.at[to], o_rsem.at[to], mate).wait_send()
        rcopy(grecv.at[to], grecv.at[to], g_ssem.at[to], g_rsem.at[to], mate).wait_send()

    loop(1, 8, chips_sent)
    for copy in (up_mate, up_other, up_both, hid_other, pair_att, pair_act, pair_gf):
        copy.wait_send()

    @pl.when(s > 0)
    def _():
        up_top.wait_send()

    @pl.when(s < N - 1)
    def _():
        up_bottom.wait_send()

    @pl.when(has_far)
    def _():
        hid_far.wait_send()

    gf_out.wait()
    out_out.wait()

    def take_pieces(k):
        t = lax.rem(s + k, N)
        g = rcopy(piece.at[t], precv.at[t], p_ssem.at[k], p_rsem.at[t], {"space": t})
        g.wait_send()
        g.wait_recv()

    loop(1, N, take_pieces)
    for side in range(2):
        total = precv[side].astype(F32)
        for i in range(1, 8):
            total += precv[2 * i + side].astype(F32)
        piece32[...] = total
        for q in range(2):
            gc_ref[pl.ds(2 * side + q, 18, stride=4), :] = piece32[pl.ds(q, 18, stride=2), :]

    def take_opieces(k):
        t = lax.rem(s + k, N)
        o = rcopy(opiece.at[t], oprecv.at[t], op_ssem.at[k], op_rsem.at[t], {"space": t})
        o.wait_send()
        o.wait_recv()

    loop(1, N, take_opieces)
    go_ref[...] = jnp.sum(oprecv[...], axis=0)


def hand_on(*refs):
    ins, outs, kept, sem = refs[:4], refs[4:8], refs[8:12], refs[12]
    first = [pltpu.make_async_copy(a, b, sem.at[0, i]) for i, (a, b) in enumerate(zip(ins, kept))]
    then = [pltpu.make_async_copy(a, b, sem.at[1, i]) for i, (a, b) in enumerate(zip(kept, outs))]
    for copy in first:
        copy.start()
    for came, goes in zip(first, then):
        came.wait()
        goes.start()
    for copy in then:
        copy.wait()


def time_features(timestep):
    halfway = TFEAT // 2
    frequency = jnp.exp(-math.log(10000.0) * jnp.arange(halfway, dtype=F32) / halfway)
    angles = timestep.astype(F32)[:, None] * frequency[None, :]
    return jnp.concatenate([jnp.cos(angles), jnp.sin(angles)], axis=1)


def on_device(features, timestep, w_time, w_emb, w_qkv, w_out, w_conv, upstream):
    tfeat = jnp.broadcast_to(time_features(timestep), (8, TFEAT))
    vmem = pl.BlockSpec(memory_space=pltpu.VMEM)
    hbm = pl.BlockSpec(memory_space=pl.ANY)
    V = pltpu.VMEM
    dma = pltpu.SemaphoreType.DMA
    scratch = [
        V((CELLS, W), BF16), V((TFEAT, W), BF16), V((W, 2 * W), BF16), V((W, 3 * W), BF16),
        V((W, W), BF16), V((9 * W, W), BF16),
        V((N, 8, 128), F32), V((N, 8, 128), F32), V((N, 8, 128), F32),
        V((8, CELLS, 128), BF16), V((8, 128, 128), BF16), V((N, CELLS, 128), BF16), V((8, 128, 128), BF16),
        V((8, CELLS, 128), BF16), V((N, CELLS, 128), BF16), V((8, CELLS, 128), F32), V((8, CELLS, 128), F32),
        V((8, 128, 128), BF16), V((8, 128, 128), BF16), V((CELLS, W), BF16),
        V((384, W), BF16), V((384, HALF), BF16), V((4, 384, HALF), BF16), V((384, 3 * W), BF16),
        V((4, 384, 3 * HALF), BF16),
        V((CELLS, W), BF16), V((CELLS, W), BF16), V((64, W), BF16), V((384, W), BF16), V((CELLS, W), BF16),
        V((384, 3 * W), BF16), V((CELLS, W), BF16), V((CELLS, W), BF16), V((CELLS, W), BF16),
        V((W, 4 * CELLS), BF16), V((W, 2 * CELLS), BF16),
        V((CELLS, W), BF16), V((CELLS, W), F32), V((CELLS, W), F32), V((CELLS, W), F32), V((CELLS, W), F32),
        V((8, 2 * W), F32),
        V((9 * W, HALF), BF16), V((8, 288, HALF), BF16), V((W, W), BF16), V((8, 32, W), BF16),
        V((288, HALF), F32), V((48, 128), F32), V((N, 48, 128), BF16), V((N, 48, 128), BF16),
        V((N, 8, 128), F32), V((N, 8, 128), F32),
        dma((9,)),
        dma((3, N)), dma((3, N)),
        dma((8,)), dma((N,)), dma((8,)), dma((8,)), dma((8,)), dma((8,)), dma((8,)),
        dma((3,)), dma((3,)), dma((7,)), dma((7,)),
        dma((8,)), dma((8,)), dma((8,)), dma((8,)), dma((N,)), dma((N,)), dma((N,)), dma((N,)),
    ]
    shapes = (
        jax.ShapeDtypeStruct((CELLS, W), BF16),
        jax.ShapeDtypeStruct((CELLS, W), BF16),
        jax.ShapeDtypeStruct((72, 128), F32),
        jax.ShapeDtypeStruct((8, 128), F32),
    )
    made = pl.pallas_call(
        kernel,
        out_shape=shapes,
        in_specs=[hbm, vmem, hbm, hbm, hbm, hbm, hbm, hbm],
        out_specs=(hbm, hbm, vmem, vmem),
        scratch_shapes=scratch,
        compiler_params=pltpu.CompilerParams(
            collective_id=0, has_side_effects=True, vmem_limit_bytes=60 * 1024 * 1024
        ),
    )(
        features.reshape(CELLS, W), tfeat, upstream.reshape(CELLS, W),
        w_time, w_emb, w_qkv, w_out, w_conv,
    )
    out, gf, gc, go = pl.pallas_call(
        hand_on,
        out_shape=shapes,
        in_specs=[hbm] * 4,
        out_specs=(hbm,) * 4,
        scratch_shapes=[V(shape.shape, shape.dtype) for shape in shapes] + [dma((2, 4))],
    )(*made)
    return (
        out.reshape(features.shape),
        gf.reshape(features.shape),
        gc.reshape(-1),
        go.reshape(-1),
    )


def solution(mesh):
    return jax.shard_map(
        on_device,
        mesh=mesh,
        in_specs=(
            P("dp", "space", None, None), P("dp"), P(), P(), P(), P(), P(),
            P("dp", "space", None, None),
        ),
        out_specs=(
            P("dp", "space", None, None), P("dp", "space", None, None),
            P(("dp", "space")), P(("dp", "space")),
        ),
        check_vma=False,
    )
```

```python
import functools
import math

import jax
import jax.numpy as jnp
from jax import lax
from jax.experimental import pallas as pl
from jax.experimental.pallas import tpu as pltpu
from jax.sharding import PartitionSpec as P

MESH = pl.DeviceIdType.MESH
F32 = jnp.float32
BF16 = jnp.bfloat16
EPS = 1e-05
LOG2E = 1.4426950408889634
TFEAT = 128
N = 16
CELLS = 256
W = 512
HALF = 256
NEAR = (0, 1, 7, 2, 6, 3, 5, 4)


def rcopy(src, dst, ssem, rsem, dev):
    return pltpu.make_async_remote_copy(
        src_ref=src, dst_ref=dst, send_sem=ssem, recv_sem=rsem, device_id=dev, device_id_type=MESH
    )


def loop(lo, hi, fn):
    def body(k, carry):
        fn(k)
        return carry

    lax.fori_loop(lo, hi, body, 0)


def far_first(i):
    return 8 + jnp.where(lax.rem(i, 2) == 1, i // 2, -(i // 2))


def share_start(buf, ssem, rsem, s):
    def go(i):
        k = far_first(i)
        t = lax.rem(s + k, N)
        rcopy(buf.at[s], buf.at[s], ssem.at[k], rsem.at[s], {"space": t}).start()

    loop(1, N, go)


def share_wait(buf, ssem, rsem, s):
    def go(k):
        t = lax.rem(s + k, N)
        copy = rcopy(buf.at[t], buf.at[t], ssem.at[k], rsem.at[t], {"space": t})
        copy.wait_send()
        copy.wait_recv()

    loop(1, N, go)


def group_sum(v):
    lane = lax.broadcasted_iota(jnp.int32, v.shape, 1)
    for k in (1, 2, 4, 8):
        v = v + jnp.where((lane & k) == 0, pltpu.roll(v, 128 - k, 1), pltpu.roll(v, k, 1))
    return v


def pack(a, b):
    return jnp.concatenate(
        [a[:, 128 * q : 128 * q + 128] for q in range(4)]
        + [b[:, 128 * q : 128 * q + 128] for q in range(4)],
        axis=0,
    )


def unpack(v, first=0):
    return jnp.concatenate([v[first + q : first + q + 1, :] for q in range(4)], axis=1)


def local_moments(values):
    mu = jnp.sum(values, axis=0, keepdims=True) / CELLS
    off = values - mu
    return pack(mu, jnp.sum(off * off, axis=0, keepdims=True))


def moments(buf):
    every = buf[...]
    total = jnp.sum(every, axis=0)
    mean = group_sum(total) / 256.0
    off = every - mean[None]
    spread = jnp.sum(off * off, axis=0) * CELLS + pltpu.roll(total, 4, 0)
    inverse = lax.rsqrt(group_sum(spread) / 65536.0 + EPS)
    return unpack(mean), unpack(inverse)


def dot(a, b):
    return jnp.dot(a, b, preferred_element_type=F32)


def dot_nt(a, b):
    return lax.dot_general(a, b, (((1,), (1,)), ((), ())), preferred_element_type=F32)


def exact_dot(v, w):
    high = v.astype(BF16)
    rest = v - high.astype(F32)
    mid = rest.astype(BF16)
    low = (rest - mid.astype(F32)).astype(BF16)
    return dot(high, w) + dot(mid, w) + dot(low, w)


def windows(v, dst):
    col = lax.broadcasted_iota(jnp.int32, v.shape, 0) & 63
    height, width = v.shape
    dst[:, 0:width] = jnp.where(col != 0, pltpu.roll(v, 1, 0), 0.0).astype(BF16)
    dst[:, width : 2 * width] = v.astype(BF16)
    dst[:, 2 * width : 3 * width] = jnp.where(col != 63, pltpu.roll(v, height - 1, 0), 0.0).astype(
        BF16
    )


def silu(v):
    return v * jax.nn.sigmoid(v)


def kernel(
    x_hbm, tf_ref, up_hbm, wtime_hbm, wemb_hbm, wqkv_hbm, wout_hbm, wconv_hbm,
    out_hbm, gf_hbm, gc_ref, go_ref,
    x_ref, wtime, wemb, wqkv, wout, wconv,
    st1, st2, st3,
    kvs, qs, kvr, qr, qq, val, top, acc, score, ats, atr, att,
    upp, uo, uh, umat, umat4,
    hid, hx, hfar, actp, xact, amat, patt, gf_ref, pgf, actt, attt,
    out_ref, hat, zed, back, thr, mod,
    gst, grecv, gost, gorecv, sum2, piece32, piece, precv, opiece, oprecv,
    lsem,
    st_ssem, st_rsem,
    kv_ssem, kv_rsem, fw_ssem, q_ssem, q_rsem, at_ssem, at_rsem,
    halo_ssem, halo_rsem, pair_ssem, pair_rsem,
    g_ssem, g_rsem, o_ssem, o_rsem, p_ssem, p_rsem, op_ssem, op_rsem,
):
    d = lax.axis_index("dp")
    s = lax.axis_index("space")
    z = s // 2
    xl = lax.rem(s, 2)
    chip = d // 2
    core = lax.rem(d, 2)
    mate = {"dp": 2 * chip + 1 - core}
    other = {"space": 2 * z + 1 - xl}

    loads = [
        pltpu.make_async_copy(a, b, lsem.at[i])
        for i, (a, b) in enumerate(
            (
                (x_hbm, x_ref),
                (wqkv_hbm, wqkv),
                (up_hbm, upp.at[pl.ds(64, CELLS)]),
                (wtime_hbm, wtime),
                (wemb_hbm, wemb),
                (wconv_hbm, wconv),
                (wout_hbm, wout),
            )
        )
    ]
    loads[0].start()
    loads[1].start()

    barrier = pltpu.get_barrier_semaphore()

    def greet(dev):
        pl.semaphore_signal(barrier, inc=1, device_id=dev, device_id_type=MESH)

    loop(1, N, lambda i: greet({"space": lax.rem(s + far_first(i), N)}))
    loop(1, 8, lambda k: greet({"dp": 2 * lax.rem(chip + k, 8) + core}))
    greet(mate)

    blank = jnp.zeros((64, W), BF16)

    @pl.when(s == 0)
    def _():
        upp[0:64, :] = blank

    @pl.when(s == N - 1)
    def _():
        upp[320:384, :] = blank

    loads[0].wait()
    st1[s] = local_moments(x_ref[...].astype(F32))
    for load in loads[2:]:
        load.start()
    pl.semaphore_wait(barrier, 15 + 7 + 1)
    share_start(st1, st_ssem.at[0], st_rsem.at[0], s)

    loads[2].wait()
    up_top = rcopy(
        upp.at[pl.ds(64, 64)], upp.at[pl.ds(320, 64)], halo_ssem.at[0], halo_rsem.at[0],
        {"space": jnp.maximum(s - 1, 0)},
    )
    up_bottom = rcopy(
        upp.at[pl.ds(256, 64)], upp.at[pl.ds(0, 64)], halo_ssem.at[1], halo_rsem.at[1],
        {"space": jnp.minimum(s + 1, N - 1)},
    )

    @pl.when(s > 0)
    def _():
        up_top.start()

    @pl.when(s < N - 1)
    def _():
        up_bottom.start()


    loads[1].wait()
    share_wait(st1, st_ssem.at[0], st_rsem.at[0], s)
    mean1, inverse1 = moments(st1)
    normed = ((x_ref[...].astype(F32) - mean1) * inverse1).astype(BF16)
    low_half = lax.broadcasted_iota(jnp.int32, (CELLS, 128), 1) < 64
    low_short = lax.broadcasted_iota(jnp.int32, (128, 128), 1) < 64
    for pair in range(4):
        q = dot(normed, wqkv[:, 128 * pair : 128 * pair + 128])
        q = q.astype(BF16).astype(F32) * 0.125
        turned = pltpu.roll(q, 64, 1)
        qs[2 * pair] = jnp.where(low_short, q[0:128], turned[128:256]).astype(BF16)
        qs[2 * pair + 1] = jnp.where(low_short, turned[0:128], q[128:256]).astype(BF16)

    def q_copy(p):
        h = lax.rem(z + NEAR[p], 8)
        slot = NEAR.index((8 - NEAR[p]) % 8)
        return rcopy(
            qs.at[h], qr.at[slot], q_ssem.at[p], q_rsem.at[slot], {"space": 2 * h + xl}
        )

    def kv_copy(p):
        h = lax.rem(z + NEAR[p], 8)
        slot = NEAR.index((8 - NEAR[p]) % 8)
        return rcopy(
            kvs.at[h], kvr.at[slot], kv_ssem.at[p], kv_rsem.at[slot], {"space": 2 * h + xl}
        )

    def forward(p):
        return rcopy(kvr.at[p], kvr.at[8 + p], fw_ssem.at[p], kv_rsem.at[8 + p], other)

    for p in range(1, 8):
        q_copy(p).start()
    for pair in range(4):
        k = dot(normed, wqkv[:, W + 128 * pair : W + 128 * pair + 128])
        v = dot(normed, wqkv[:, 2 * W + 128 * pair : 2 * W + 128 * pair + 128])
        kvs[2 * pair] = jnp.where(low_half, k, pltpu.roll(v, 64, 1)).astype(BF16)
        kvs[2 * pair + 1] = jnp.where(low_half, pltpu.roll(k, 64, 1), v).astype(BF16)
    for p in (1, 2):
        kv_copy(p).start()
    kvr[0] = kvs[z]
    qr[0] = qs[z]
    forward(0).start()

    loads[3].wait()
    loads[4].wait()
    embedded = exact_dot(jnp.broadcast_to(tf_ref[...], (8, TFEAT)), wtime[...])
    mod[...] = exact_dot(silu(embedded), wemb[...])

    @pl.when(s < N - 1)
    def _():
        up_top.wait_recv()

    @pl.when(s > 0)
    def _():
        up_bottom.wait_recv()

    uh[0] = upp[:, pl.ds(pl.multiple_of(HALF * xl, HALF), HALF)]
    uo[...] = upp[:, pl.ds(pl.multiple_of(HALF * (1 - xl), HALF), HALF)]
    up_mate = rcopy(uh.at[0], uh.at[2], pair_ssem.at[0], pair_rsem.at[0], mate)
    up_other = rcopy(uo, uh.at[1], pair_ssem.at[1], pair_rsem.at[1], other)
    up_both = rcopy(uh.at[1], uh.at[3], pair_ssem.at[2], pair_rsem.at[2], mate)
    up_mate.start()
    windows(upp[...].astype(F32), umat)
    windows(uh[0].astype(F32), umat4.at[0])
    loads[5].wait()
    loads[6].wait()
    back[...] = jnp.zeros_like(back)
    kv_copy(3).start()
    kv_copy(4).start()

    def back_step(p):
        a = p // 3
        b = lax.rem(p, 3)
        rows = pl.ds(pl.multiple_of(64 * (2 - a), 64), CELLS)
        lanes = pl.ds(pl.multiple_of(W * (2 - b), W), W)
        back[...] += dot_nt(umat[rows, lanes], wconv[pl.ds(pl.multiple_of(W * p, W), W), :])

    loop(0, 9, back_step)

    for p in range(1, 8):
        q_copy(NEAR.index((8 - NEAR[p]) % 8)).wait_recv()
    kv_copy(5).start()
    kv_copy(6).start()
    for p in range(8):
        q = qr[p].astype(F32)
        qq[p, 0:128, :] = jnp.where(low_short, q, 0.0).astype(BF16)
        qq[p, 128:256, :] = jnp.where(low_short, pltpu.roll(q, 64, 1), 0.0).astype(BF16)

    def take(p):
        if 1 <= p < 8:
            kv_copy(NEAR.index((8 - NEAR[p]) % 8)).wait_recv()
            forward(p).start()
        if p >= 8:
            forward(p - 8).wait_recv()
        val[p] = jnp.where(low_half, 1.0, kvr[p].astype(F32)).astype(BF16)

    def scores(i, slots, b):
        for j, p in enumerate(slots):
            score[b, j] = dot_nt(qq[i], kvr[p])

    def attend(i, slots, b, first, last):
        high = None
        for j in range(len(slots)):
            part = jnp.maximum(score[b, j, :, 0:128], score[b, j, :, 128:256])
            high = part if high is None else jnp.maximum(high, part)
        high = jnp.max(high, axis=1, keepdims=True) * LOG2E
        if not first:
            before = top[i]
            high = jnp.maximum(before, high)
        else:
            high = jnp.broadcast_to(high, (CELLS, 128))
        wide = jnp.concatenate([high, high], axis=1)
        total = None
        for j, p in enumerate(slots):
            mixed = dot(jnp.exp2(score[b, j] * LOG2E - wide).astype(BF16), val[p])
            total = mixed if total is None else total + mixed
        if not first:
            total = total + acc[i] * jnp.exp2(before - high)
        if not last:
            top[i] = high
            acc[i] = total
        return total

    def finish(total):
        ratio = total / pltpu.roll(total, 64, 1)
        return jnp.where(low_short, pltpu.roll(ratio[0:128], 64, 1), ratio[128:256]).astype(BF16)

    def go(*slots):
        first, last = 0 in slots, 15 in slots

        def use(i, b):
            total = attend(i, slots, b, first, last)
            if last:
                ats[i] = finish(total)

                @pl.when(i > 0)
                def _():
                    away = jnp.where(lax.rem(i, 2) == 1, (i + 1) // 2, 8 - i // 2)
                    there = 2 * lax.rem(z + away, 8) + xl
                    rcopy(
                        ats.at[i], atr.at[z], at_ssem.at[i], at_rsem.at[z], {"space": there}
                    ).start()

        def turn(k):
            return 7 - k if last else k

        def step(m):
            k = 2 * m
            scores(turn(k + 1), slots, 1)
            use(turn(k), 0)
            scores(turn(jnp.minimum(k + 2, 7)), slots, 0)
            use(turn(k + 1), 1)

        scores(turn(0), slots, 0)
        loop(0, 4, step)

    take(0)
    take(8)
    take(1)
    take(2)
    kv_copy(7).start()
    go(0, 8, 1, 2)
    take(3)
    take(4)
    take(9)
    take(10)
    go(3, 4, 9, 10)
    take(5)
    take(6)
    take(11)
    take(12)
    go(5, 6, 11, 12)
    for p in (7, 13, 14, 15):
        take(p)
    up_other.start()
    go(7, 13, 14, 15)
    atr[z] = ats[0]

    for k in range(1, 8):
        h = lax.rem(z + k, 8)
        rcopy(ats.at[k], atr.at[h], at_ssem.at[k], at_rsem.at[h], other).wait_recv()
    for pair in range(4):
        first = atr[2 * pair].astype(F32)
        second = atr[2 * pair + 1].astype(F32)
        lanes = slice(128 * pair, 128 * pair + 128)
        att[0:128, lanes] = jnp.where(low_short, first, pltpu.roll(second, 64, 1)).astype(BF16)
        att[128:256, lanes] = jnp.where(low_short, pltpu.roll(first, 64, 1), second).astype(BF16)

    hidden = (x_ref[...].astype(F32) + dot(att[...], wout[...])).astype(BF16)
    hid[...] = hidden
    hidden = hidden.astype(F32)
    st2[s] = local_moments(hidden)
    share_start(st2, st_ssem.at[1], st_rsem.at[1], s)
    far = s - 1 + 2 * xl
    has_far = (far >= 0) & (far < N)
    hid_far = rcopy(
        hid.at[pl.ds(pl.multiple_of(192 * xl, 64), 64)], hfar, halo_ssem.at[2], halo_rsem.at[2],
        {"space": jnp.clip(far, 0, N - 1)},
    )

    @pl.when(has_far)
    def _():
        hid_far.start()

    hid_other = rcopy(hid, hx, pair_ssem.at[3], pair_rsem.at[3], other)
    hid_other.start()
    pair_att = rcopy(att, patt, pair_ssem.at[4], pair_rsem.at[4], mate)
    pair_att.start()
    up_other.wait_recv()
    up_both.start()
    windows(uh[1].astype(F32), umat4.at[1])
    up_mate.wait_recv()
    windows(uh[2].astype(F32), umat4.at[2])
    up_both.wait_recv()
    windows(uh[3].astype(F32), umat4.at[3])
    attt[:, 0:CELLS] = att[...].T
    pair_att.wait_recv()
    attt[:, CELLS : 2 * CELLS] = patt[...].T

    share_wait(st2, st_ssem.at[1], st_rsem.at[1], s)
    mean2, inverse2 = moments(st2)
    scale = 1.0 + mod[0:1, 0:W]
    shift = mod[0:1, W : 2 * W]
    gain = inverse2 * scale

    def act_of(ref):
        return silu((ref[...].astype(F32) - mean2) * inverse2 * scale + shift).astype(BF16)

    hats = (hid[...].astype(F32) - mean2) * inverse2
    hat[...] = hats
    shifted = hats * scale + shift
    sigma = jax.nn.sigmoid(shifted)
    act = (shifted * sigma).astype(BF16)
    actp[64:320, :] = act
    actt[:, 0:CELLS] = act.T
    hid_other.wait_recv()
    xact[...] = act_of(hx)
    actt[:, CELLS : 2 * CELLS] = xact[...].T
    pair_act = rcopy(
        actt.at[:, pl.ds(0, 2 * CELLS)], actt.at[:, pl.ds(2 * CELLS, 2 * CELLS)],
        pair_ssem.at[5], pair_rsem.at[5], mate,
    )
    pair_act.start()

    through = back[...] * sigma * (1.0 + shifted * (1.0 - sigma)) * scale
    thr[...] = through
    st3[s] = pack(
        jnp.sum(through, axis=0, keepdims=True),
        jnp.sum(through * hats, axis=0, keepdims=True),
    )
    share_start(st3, st_ssem.at[2], st_rsem.at[2], s)

    actp[pl.ds(pl.multiple_of(320 * (1 - xl), 64), 64), :] = xact[
        pl.ds(pl.multiple_of(192 * xl, 64), 64), :
    ]
    edge = pl.ds(pl.multiple_of(320 * xl, 64), 64)

    @pl.when(has_far)
    def _():
        hid_far.wait_recv()
        actp[edge, :] = act_of(hfar)

    @pl.when(jnp.logical_not(has_far))
    def _():
        actp[edge, :] = blank

    windows(actp[...].astype(F32), amat)
    pair_act.wait_recv()

    def grad_copy(half, to):
        return rcopy(
            gst.at[pl.ds(pl.multiple_of(576 * to + 288 * core + 144 * half, 16), 144)],
            grecv.at[chip, pl.ds(144 * half, 144)],
            g_ssem.at[half, to],
            g_rsem.at[half, chip],
            {"dp": 2 * to + core},
        )

    def grad_step(j):
        p = lax.rem(chip + 1 + j, 9)
        a = p // 3
        b = lax.rem(p, 3)
        rows = pl.ds(pl.multiple_of(64 * (2 - a), 64), CELLS)
        lanes = pl.ds(pl.multiple_of(HALF * (2 - b), HALF), HALF)
        part = dot(actt[:, 0:CELLS], umat4[0, rows, lanes])
        for i in range(1, 4):
            part += dot(actt[:, CELLS * i : CELLS * i + CELLS], umat4[i, rows, lanes])
        gst[pl.ds(pl.multiple_of(W * p, W), W), :] = part.astype(BF16)

        @pl.when((j >= 1) & (p >= 1))
        def _():
            grad_copy(0, p - 1).start()

    loop(0, 9, grad_step)

    share_wait(st3, st_ssem.at[2], st_rsem.at[2], s)
    sums = group_sum(jnp.sum(st3[...], axis=0)) / 65536.0
    gf_ref[...] = (inverse2 * (thr[...] - unpack(sums) - hat[...] * unpack(sums, 4))).astype(BF16)
    pair_gf = rcopy(gf_ref, pgf, pair_ssem.at[6], pair_rsem.at[6], mate)
    pair_gf.start()
    gf_out = pltpu.make_async_copy(gf_ref, gf_hbm, lsem.at[7])
    gf_out.start()
    part = dot(attt[:, 0:CELLS], gf_ref[...])
    pair_gf.wait_recv()
    gost[...] = (part + dot(attt[:, CELLS : 2 * CELLS], pgf[...])).astype(BF16)

    def send_out(k):
        to = lax.rem(chip + k, 8)
        rcopy(
            gost.at[pl.ds(pl.multiple_of(64 * to + 32 * core, 32), 32)],
            gorecv.at[chip],
            o_ssem.at[to],
            o_rsem.at[chip],
            {"dp": 2 * to + core},
        ).start()

    loop(1, 8, send_out)
    loop(1, 8, lambda k: grad_copy(1, lax.rem(chip + k, 8)).start())

    thr[...] = jnp.zeros_like(thr)

    def conv_step(a):
        thr[...] += dot(
            amat[pl.ds(pl.multiple_of(64 * a, 64), CELLS), :],
            wconv[pl.ds(pl.multiple_of(3 * W * a, W), 3 * W), :],
        )

    loop(0, 3, conv_step)
    out_ref[...] = thr[...].astype(BF16)
    out_out = pltpu.make_async_copy(out_ref, out_hbm, lsem.at[8])
    out_out.start()

    def second(half):
        def take_grad(k):
            frm = lax.rem(chip + k, 8)
            part = grecv.at[frm, pl.ds(144 * half, 144)]
            rcopy(part, part, g_ssem.at[half, frm], g_rsem.at[half, frm], mate).wait_recv()

        loop(1, 8, take_grad)
        grecv[chip, 144 * half : 144 * half + 144] = gst[
            pl.ds(pl.multiple_of(576 * chip + 288 * core + 144 * half, 16), 144), :
        ]
        sum2[...] = jnp.sum(grecv[:, 144 * half : 144 * half + 144].astype(F32), axis=0)
        for i in range(8):
            t = 8 * half + i
            for q in range(2):
                piece32[pl.ds(q, 18, stride=2), :] = sum2[
                    18 * i : 18 * i + 18, 128 * q : 128 * q + 128
                ]
            piece[t] = piece32[...].astype(BF16)

        def send_piece(i):
            t = 8 * half + i

            @pl.when(t != s)
            def _():
                rcopy(piece.at[t], precv.at[s], p_ssem.at[t], p_rsem.at[s], {"space": t}).start()

            @pl.when(t == s)
            def _():
                precv[s] = piece[s]

        loop(0, 8, send_piece)

    piece32[...] = jnp.zeros_like(piece32)
    second(0)

    def take_out(k):
        frm = lax.rem(chip + k, 8)
        rcopy(gorecv.at[frm], gorecv.at[frm], o_ssem.at[frm], o_rsem.at[frm], mate).wait_recv()

    loop(1, 8, take_out)
    gorecv[chip] = gost[pl.ds(pl.multiple_of(64 * chip + 32 * core, 32), 32), :]
    out_sum = jnp.sum(gorecv[...].astype(F32), axis=0)
    for t in range(N):
        opiece[t] = pack(out_sum[2 * t : 2 * t + 1], out_sum[2 * t + 1 : 2 * t + 2])

    def send_opiece(k):
        t = lax.rem(s + k, N)
        rcopy(opiece.at[t], oprecv.at[s], op_ssem.at[k], op_rsem.at[s], {"space": t}).start()

    loop(1, N, send_opiece)
    oprecv[s] = opiece[s]
    second(1)

    for p in range(8):
        forward(p).wait_send()
        if p:
            kv_copy(p).wait_send()
            q_copy(p).wait_send()
            rcopy(ats.at[p], atr.at[0], at_ssem.at[p], at_rsem.at[0], other).wait_send()

    def chips_sent(k):
        to = lax.rem(chip + k, 8)
        rcopy(gorecv.at[to], gorecv.at[to], o_ssem.at[to], o_rsem.at[to], mate).wait_send()
        grad_copy(0, to).wait_send()
        grad_copy(1, to).wait_send()

    loop(1, 8, chips_sent)
    for copy in (up_mate, up_other, up_both, hid_other, pair_att, pair_act, pair_gf):
        copy.wait_send()

    @pl.when(s > 0)
    def _():
        up_top.wait_send()

    @pl.when(s < N - 1)
    def _():
        up_bottom.wait_send()

    @pl.when(has_far)
    def _():
        hid_far.wait_send()

    gf_out.wait()
    out_out.wait()

    def take_pieces(k):
        t = lax.rem(s + k, N)
        g = rcopy(piece.at[t], precv.at[t], p_ssem.at[t], p_rsem.at[t], {"space": t})
        g.wait_send()
        g.wait_recv()

    loop(1, N, take_pieces)
    for side in range(2):
        total = precv[side].astype(F32)
        for i in range(1, 8):
            total += precv[2 * i + side].astype(F32)
        piece32[...] = total
        for q in range(2):
            gc_ref[pl.ds(2 * side + q, 18, stride=4), :] = piece32[pl.ds(q, 18, stride=2), :]

    def take_opieces(k):
        t = lax.rem(s + k, N)
        o = rcopy(opiece.at[t], oprecv.at[t], op_ssem.at[k], op_rsem.at[t], {"space": t})
        o.wait_send()
        o.wait_recv()

    loop(1, N, take_opieces)
    go_ref[...] = jnp.sum(oprecv[...], axis=0)


def hand_on(*refs):
    ins, outs, kept, sem = refs[:4], refs[4:8], refs[8:12], refs[12]
    first = [pltpu.make_async_copy(a, b, sem.at[0, i]) for i, (a, b) in enumerate(zip(ins, kept))]
    then = [pltpu.make_async_copy(a, b, sem.at[1, i]) for i, (a, b) in enumerate(zip(kept, outs))]
    for copy in first:
        copy.start()
    for came, goes in zip(first, then):
        came.wait()
        goes.start()
    for copy in then:
        copy.wait()


def time_features(timestep):
    halfway = TFEAT // 2
    frequency = jnp.exp(-math.log(10000.0) * jnp.arange(halfway, dtype=F32) / halfway)
    angles = timestep.astype(F32)[:, None] * frequency[None, :]
    return jnp.concatenate([jnp.cos(angles), jnp.sin(angles)], axis=1)


def on_device(features, timestep, w_time, w_emb, w_qkv, w_out, w_conv, upstream):
    tfeat = time_features(timestep)
    vmem = pl.BlockSpec(memory_space=pltpu.VMEM)
    hbm = pl.BlockSpec(memory_space=pl.ANY)
    V = pltpu.VMEM
    dma = pltpu.SemaphoreType.DMA
    scratch = [
        V((CELLS, W), BF16), V((TFEAT, W), BF16), V((W, 2 * W), BF16), V((W, 3 * W), BF16),
        V((W, W), BF16), V((9 * W, W), BF16),
        V((N, 8, 128), F32), V((N, 8, 128), F32), V((N, 8, 128), F32),
        V((8, CELLS, 128), BF16), V((8, 128, 128), BF16), V((N, CELLS, 128), BF16), V((8, 128, 128), BF16),
        V((8, CELLS, 128), BF16), V((N, CELLS, 128), BF16), V((8, CELLS, 128), F32), V((8, CELLS, 128), F32),
        V((2, 4, CELLS, CELLS), F32), V((8, 128, 128), BF16), V((8, 128, 128), BF16), V((CELLS, W), BF16),
        V((384, W), BF16), V((384, HALF), BF16), V((4, 384, HALF), BF16), V((384, 3 * W), BF16),
        V((4, 384, 3 * HALF), BF16),
        V((CELLS, W), BF16), V((CELLS, W), BF16), V((64, W), BF16), V((384, W), BF16), V((CELLS, W), BF16),
        V((384, 3 * W), BF16), V((CELLS, W), BF16), V((CELLS, W), BF16), V((CELLS, W), BF16),
        V((W, 4 * CELLS), BF16), V((W, 2 * CELLS), BF16),
        V((CELLS, W), BF16), V((CELLS, W), F32), V((CELLS, W), F32), V((CELLS, W), F32), V((CELLS, W), F32),
        V((8, 2 * W), F32),
        V((9 * W, HALF), BF16), V((8, 288, HALF), BF16), V((W, W), BF16), V((8, 32, W), BF16),
        V((144, HALF), F32), V((48, 128), F32), V((N, 48, 128), BF16), V((N, 48, 128), BF16),
        V((N, 8, 128), F32), V((N, 8, 128), F32),
        dma((9,)),
        dma((3, N)), dma((3, N)),
        dma((8,)), dma((N,)), dma((8,)), dma((8,)), dma((8,)), dma((8,)), dma((8,)),
        dma((3,)), dma((3,)), dma((7,)), dma((7,)),
        dma((2, 8)), dma((2, 8)), dma((8,)), dma((8,)), dma((N,)), dma((N,)), dma((N,)), dma((N,)),
    ]
    shapes = (
        jax.ShapeDtypeStruct((CELLS, W), BF16),
        jax.ShapeDtypeStruct((CELLS, W), BF16),
        jax.ShapeDtypeStruct((72, 128), F32),
        jax.ShapeDtypeStruct((8, 128), F32),
    )
    made = pl.pallas_call(
        kernel,
        out_shape=shapes,
        in_specs=[hbm, vmem, hbm, hbm, hbm, hbm, hbm, hbm],
        out_specs=(hbm, hbm, vmem, vmem),
        scratch_shapes=scratch,
        compiler_params=pltpu.CompilerParams(
            collective_id=0, has_side_effects=True, vmem_limit_bytes=60 * 1024 * 1024
        ),
    )(
        features.reshape(CELLS, W), tfeat, upstream.reshape(CELLS, W),
        w_time, w_emb, w_qkv, w_out, w_conv,
    )
    out, gf, gc, go = pl.pallas_call(
        hand_on,
        out_shape=shapes,
        in_specs=[hbm] * 4,
        out_specs=(hbm,) * 4,
        scratch_shapes=[V(shape.shape, shape.dtype) for shape in shapes] + [dma((2, 4))],
    )(*made)
    return (
        out.reshape(features.shape),
        gf.reshape(features.shape),
        gc.reshape(-1),
        go.reshape(-1),
    )


def solution(mesh):
    return jax.shard_map(
        on_device,
        mesh=mesh,
        in_specs=(
            P("dp", "space", None, None), P("dp"), P(), P(), P(), P(), P(),
            P("dp", "space", None, None),
        ),
        out_specs=(
            P("dp", "space", None, None), P("dp", "space", None, None),
            P(("dp", "space")), P(("dp", "space")),
        ),
        check_vma=False,
    )
```

```python
import functools
import math

import jax
import jax.numpy as jnp
from jax import lax
from jax.experimental import pallas as pl
from jax.experimental.pallas import tpu as pltpu
from jax.sharding import PartitionSpec as P

MESH = pl.DeviceIdType.MESH
F32 = jnp.float32
BF16 = jnp.bfloat16
EPS = 1e-05
LOG2E = 1.4426950408889634
TFEAT = 128
N = 16
CELLS = 256
W = 512
HALF = 256
NEAR = (0, 1, 7, 2, 6, 3, 5, 4)


def rcopy(src, dst, ssem, rsem, dev):
    return pltpu.make_async_remote_copy(
        src_ref=src, dst_ref=dst, send_sem=ssem, recv_sem=rsem, device_id=dev, device_id_type=MESH
    )


def loop(lo, hi, fn):
    def body(k, carry):
        fn(k)
        return carry

    lax.fori_loop(lo, hi, body, 0)


def far_first(i):
    return 8 + jnp.where(lax.rem(i, 2) == 1, i // 2, -(i // 2))


def share_start(buf, ssem, rsem, s):
    def go(i):
        k = far_first(i)
        t = lax.rem(s + k, N)
        rcopy(buf.at[s], buf.at[s], ssem.at[k], rsem.at[s], {"space": t}).start()

    loop(1, N, go)


def share_wait(buf, ssem, rsem, s):
    def go(k):
        t = lax.rem(s + k, N)
        copy = rcopy(buf.at[t], buf.at[t], ssem.at[k], rsem.at[t], {"space": t})
        copy.wait_send()
        copy.wait_recv()

    loop(1, N, go)


def group_sum(v):
    lane = lax.broadcasted_iota(jnp.int32, v.shape, 1)
    for k in (1, 2, 4, 8):
        v = v + jnp.where((lane & k) == 0, pltpu.roll(v, 128 - k, 1), pltpu.roll(v, k, 1))
    return v


def pack(a, b):
    return jnp.concatenate(
        [a[:, 128 * q : 128 * q + 128] for q in range(4)]
        + [b[:, 128 * q : 128 * q + 128] for q in range(4)],
        axis=0,
    )


def unpack(v, first=0):
    return jnp.concatenate([v[first + q : first + q + 1, :] for q in range(4)], axis=1)


def local_moments(values):
    mu = jnp.sum(values, axis=0, keepdims=True) / CELLS
    off = values - mu
    return pack(mu, jnp.sum(off * off, axis=0, keepdims=True))


def moments(buf):
    every = buf[...]
    total = jnp.sum(every, axis=0)
    mean = group_sum(total) / 256.0
    off = every - mean[None]
    spread = jnp.sum(off * off, axis=0) * CELLS + pltpu.roll(total, 4, 0)
    inverse = lax.rsqrt(group_sum(spread) / 65536.0 + EPS)
    return unpack(mean), unpack(inverse)


def dot(a, b):
    return jnp.dot(a, b, preferred_element_type=F32)


def dot_nt(a, b):
    return lax.dot_general(a, b, (((1,), (1,)), ((), ())), preferred_element_type=F32)


def exact_dot(v, w):
    high = v.astype(BF16)
    rest = v - high.astype(F32)
    mid = rest.astype(BF16)
    low = (rest - mid.astype(F32)).astype(BF16)
    return dot(high, w) + dot(mid, w) + dot(low, w)


def windows(v, dst):
    col = lax.broadcasted_iota(jnp.int32, v.shape, 0) & 63
    height, width = v.shape
    dst[:, 0:width] = jnp.where(col != 0, pltpu.roll(v, 1, 0), 0.0).astype(BF16)
    dst[:, width : 2 * width] = v.astype(BF16)
    dst[:, 2 * width : 3 * width] = jnp.where(col != 63, pltpu.roll(v, height - 1, 0), 0.0).astype(
        BF16
    )


def silu(v):
    return v * jax.nn.sigmoid(v)


def kernel(
    x_hbm, t_ref, up_hbm, wtime_hbm, wemb_hbm, wqkv_hbm, wout_hbm, wconv_hbm,
    out_hbm, gf_hbm, gc_ref, go_ref,
    x_ref, wtime, wemb, wqkv, wout, wconv,
    st1, st2, st3,
    kvs, qs, kvr, qr, qq, val, top, acc, score, ats, atr, att,
    upp, uo, uh, umat, umat4,
    hid, hx, hfar, actp, xact, amat, patt, gf_ref, pgf, actt, attt,
    out_ref, hat, zed, back, thr, mod,
    gst, grecv, gost, gorecv, sum2, piece32, piece, precv, opiece, oprecv,
    wide32, pack32, zpiece, zrecv, fpiece, frecv,
    lsem,
    st_ssem, st_rsem,
    kv_ssem, kv_rsem, fw_ssem, q_ssem, q_rsem, at_ssem, at_rsem,
    halo_ssem, halo_rsem, pair_ssem, pair_rsem,
    g_ssem, g_rsem, o_ssem, o_rsem, p_ssem, p_rsem, op_ssem, op_rsem, z_ssem, z_rsem, f_ssem, f_rsem,
):
    d = lax.axis_index("dp")
    s = lax.axis_index("space")
    z = s // 2
    xl = lax.rem(s, 2)
    chip = d // 2
    core = lax.rem(d, 2)
    mate = {"dp": 2 * chip + 1 - core}
    other = {"space": 2 * z + 1 - xl}
    afar = 2 * lax.rem(chip // 2 + 2, 4) + 1 - lax.rem(chip, 2)

    loads = [
        pltpu.make_async_copy(a, b, lsem.at[i])
        for i, (a, b) in enumerate(
            (
                (x_hbm, x_ref),
                (wqkv_hbm, wqkv),
                (up_hbm, upp.at[pl.ds(64, CELLS)]),
                (wtime_hbm, wtime),
                (wemb_hbm, wemb),
                (wconv_hbm, wconv),
                (wout_hbm, wout),
            )
        )
    ]
    loads[0].start()
    loads[1].start()

    barrier = pltpu.get_barrier_semaphore()

    def greet(dev):
        pl.semaphore_signal(barrier, inc=1, device_id=dev, device_id_type=MESH)

    loop(1, N, lambda i: greet({"space": lax.rem(s + far_first(i), N)}))
    loop(1, 8, lambda k: greet({"dp": 2 * lax.rem(chip + k, 8) + core}))
    greet(mate)
    greet({"dp": 2 * afar + core, "space": 2 * z + 1 - xl})

    blank = jnp.zeros((64, W), BF16)

    @pl.when(s == 0)
    def _():
        upp[0:64, :] = blank

    @pl.when(s == N - 1)
    def _():
        upp[320:384, :] = blank

    loads[0].wait()
    st1[s] = local_moments(x_ref[...].astype(F32))
    for load in loads[2:]:
        load.start()
    pl.semaphore_wait(barrier, 15 + 7 + 1 + 1)
    share_start(st1, st_ssem.at[0], st_rsem.at[0], s)

    loads[2].wait()
    up_top = rcopy(
        upp.at[pl.ds(64, 64)], upp.at[pl.ds(320, 64)], halo_ssem.at[0], halo_rsem.at[0],
        {"space": jnp.maximum(s - 1, 0)},
    )
    up_bottom = rcopy(
        upp.at[pl.ds(256, 64)], upp.at[pl.ds(0, 64)], halo_ssem.at[1], halo_rsem.at[1],
        {"space": jnp.minimum(s + 1, N - 1)},
    )

    @pl.when(s > 0)
    def _():
        up_top.start()

    @pl.when(s < N - 1)
    def _():
        up_bottom.start()


    loads[1].wait()
    share_wait(st1, st_ssem.at[0], st_rsem.at[0], s)
    mean1, inverse1 = moments(st1)
    normed = ((x_ref[...].astype(F32) - mean1) * inverse1).astype(BF16)
    low_half = lax.broadcasted_iota(jnp.int32, (CELLS, 128), 1) < 64
    low_short = lax.broadcasted_iota(jnp.int32, (128, 128), 1) < 64
    for pair in range(4):
        q = dot(normed, wqkv[:, 128 * pair : 128 * pair + 128])
        q = q.astype(BF16).astype(F32) * 0.125
        turned = pltpu.roll(q, 64, 1)
        qs[2 * pair] = jnp.where(low_short, q[0:128], turned[128:256]).astype(BF16)
        qs[2 * pair + 1] = jnp.where(low_short, turned[0:128], q[128:256]).astype(BF16)

    def q_copy(p):
        h = lax.rem(z + NEAR[p], 8)
        slot = NEAR.index((8 - NEAR[p]) % 8)
        return rcopy(
            qs.at[h], qr.at[slot], q_ssem.at[p], q_rsem.at[slot], {"space": 2 * h + xl}
        )

    def kv_copy(p):
        h = lax.rem(z + NEAR[p], 8)
        slot = NEAR.index((8 - NEAR[p]) % 8)
        return rcopy(
            kvs.at[h], kvr.at[slot], kv_ssem.at[p], kv_rsem.at[slot], {"space": 2 * h + xl}
        )

    def forward(p):
        return rcopy(kvr.at[p], kvr.at[8 + p], fw_ssem.at[p], kv_rsem.at[8 + p], other)

    for p in range(1, 8):
        q_copy(p).start()
    for pair in range(4):
        k = dot(normed, wqkv[:, W + 128 * pair : W + 128 * pair + 128])
        v = dot(normed, wqkv[:, 2 * W + 128 * pair : 2 * W + 128 * pair + 128])
        kvs[2 * pair] = jnp.where(low_half, k, pltpu.roll(v, 64, 1)).astype(BF16)
        kvs[2 * pair + 1] = jnp.where(low_half, pltpu.roll(k, 64, 1), v).astype(BF16)
    for p in (1, 2):
        kv_copy(p).start()
    kvr[0] = kvs[z]
    qr[0] = qs[z]
    forward(0).start()

    loads[3].wait()
    loads[4].wait()
    spot = lax.broadcasted_iota(jnp.int32, (8, TFEAT), 1)
    nth = (spot & (TFEAT // 2 - 1)).astype(F32)
    angle = t_ref[0].astype(F32) * jnp.exp(-math.log(10000.0) * nth / (TFEAT // 2))
    embedded = exact_dot(jnp.where(spot < TFEAT // 2, jnp.cos(angle), jnp.sin(angle)), wtime[...])
    mod[...] = exact_dot(silu(embedded), wemb[...])

    @pl.when(s < N - 1)
    def _():
        up_top.wait_recv()

    @pl.when(s > 0)
    def _():
        up_bottom.wait_recv()

    uh[0] = upp[:, pl.ds(pl.multiple_of(HALF * xl, HALF), HALF)]
    uo[...] = upp[:, pl.ds(pl.multiple_of(HALF * (1 - xl), HALF), HALF)]
    up_mate = rcopy(uh.at[0], uh.at[2], pair_ssem.at[0], pair_rsem.at[0], mate)
    up_other = rcopy(uo, uh.at[1], pair_ssem.at[1], pair_rsem.at[1], other)
    up_both = rcopy(uh.at[1], uh.at[3], pair_ssem.at[2], pair_rsem.at[2], mate)
    up_mate.start()
    windows(upp[...].astype(F32), umat)
    windows(uh[0].astype(F32), umat4.at[0])
    loads[5].wait()
    loads[6].wait()
    back[...] = jnp.zeros_like(back)
    kv_copy(3).start()
    kv_copy(4).start()

    def back_step(p):
        a = p // 3
        b = lax.rem(p, 3)
        rows = pl.ds(pl.multiple_of(64 * (2 - a), 64), CELLS)
        lanes = pl.ds(pl.multiple_of(W * (2 - b), W), W)
        back[...] += dot_nt(umat[rows, lanes], wconv[pl.ds(pl.multiple_of(W * p, W), W), :])

    loop(0, 9, back_step)

    for p in range(1, 8):
        q_copy(NEAR.index((8 - NEAR[p]) % 8)).wait_recv()
    kv_copy(5).start()
    kv_copy(6).start()
    for p in range(8):
        q = qr[p].astype(F32)
        qq[p, 0:128, :] = jnp.where(low_short, q, 0.0).astype(BF16)
        qq[p, 128:256, :] = jnp.where(low_short, pltpu.roll(q, 64, 1), 0.0).astype(BF16)

    def take(p):
        if 1 <= p < 8:
            kv_copy(NEAR.index((8 - NEAR[p]) % 8)).wait_recv()
            forward(p).start()
        if p >= 8:
            forward(p - 8).wait_recv()
        val[p] = jnp.where(low_half, 1.0, kvr[p].astype(F32)).astype(BF16)

    def scores(i, slots, b):
        for j, p in enumerate(slots):
            score[b, j] = dot_nt(qq[i], kvr[p])

    def attend(i, slots, b, first, last):
        high = None
        for j in range(len(slots)):
            part = jnp.maximum(score[b, j, :, 0:128], score[b, j, :, 128:256])
            high = part if high is None else jnp.maximum(high, part)
        high = jnp.max(high, axis=1, keepdims=True) * LOG2E
        if not first:
            before = top[i]
            high = jnp.maximum(before, high)
        else:
            high = jnp.broadcast_to(high, (CELLS, 128))
        wide = jnp.concatenate([high, high], axis=1)
        total = None
        for j, p in enumerate(slots):
            mixed = dot(jnp.exp2(score[b, j] * LOG2E - wide).astype(BF16), val[p])
            total = mixed if total is None else total + mixed
        if not first:
            total = total + acc[i] * jnp.exp2(before - high)
        if not last:
            top[i] = high
            acc[i] = total
        return total

    def finish(total):
        ratio = total / pltpu.roll(total, 64, 1)
        return jnp.where(low_short, pltpu.roll(ratio[0:128], 64, 1), ratio[128:256]).astype(BF16)

    def go(*slots):
        first, last = 0 in slots, 15 in slots

        def use(i, b):
            total = attend(i, slots, b, first, last)
            if last:
                ats[i] = finish(total)

                @pl.when(i > 0)
                def _():
                    away = jnp.where(lax.rem(i, 2) == 1, (i + 1) // 2, 8 - i // 2)
                    there = 2 * lax.rem(z + away, 8) + xl
                    rcopy(
                        ats.at[i], atr.at[z], at_ssem.at[i], at_rsem.at[z], {"space": there}
                    ).start()

        def turn(k):
            return 7 - k if last else k

        def step(m):
            k = 2 * m
            scores(turn(k + 1), slots, 1)
            use(turn(k), 0)
            scores(turn(jnp.minimum(k + 2, 7)), slots, 0)
            use(turn(k + 1), 1)

        scores(turn(0), slots, 0)
        loop(0, 4, step)

    take(0)
    take(8)
    take(1)
    take(2)
    kv_copy(7).start()
    go(0, 8, 1, 2)
    take(3)
    take(4)
    take(9)
    take(10)
    go(3, 4, 9, 10)
    take(5)
    take(6)
    take(11)
    take(12)
    go(5, 6, 11, 12)
    for p in (7, 13, 14, 15):
        take(p)
    up_other.start()
    go(7, 13, 14, 15)
    atr[z] = ats[0]

    for k in range(1, 8):
        h = lax.rem(z + k, 8)
        rcopy(ats.at[k], atr.at[h], at_ssem.at[k], at_rsem.at[h], other).wait_recv()
    for pair in range(4):
        first = atr[2 * pair].astype(F32)
        second = atr[2 * pair + 1].astype(F32)
        lanes = slice(128 * pair, 128 * pair + 128)
        att[0:128, lanes] = jnp.where(low_short, first, pltpu.roll(second, 64, 1)).astype(BF16)
        att[128:256, lanes] = jnp.where(low_short, pltpu.roll(first, 64, 1), second).astype(BF16)

    hidden = (x_ref[...].astype(F32) + dot(att[...], wout[...])).astype(BF16)
    hid[...] = hidden
    hidden = hidden.astype(F32)
    st2[s] = local_moments(hidden)
    share_start(st2, st_ssem.at[1], st_rsem.at[1], s)
    far = s - 1 + 2 * xl
    has_far = (far >= 0) & (far < N)
    hid_far = rcopy(
        hid.at[pl.ds(pl.multiple_of(192 * xl, 64), 64)], hfar, halo_ssem.at[2], halo_rsem.at[2],
        {"space": jnp.clip(far, 0, N - 1)},
    )

    @pl.when(has_far)
    def _():
        hid_far.start()

    hid_other = rcopy(hid, hx, pair_ssem.at[3], pair_rsem.at[3], other)
    hid_other.start()
    pair_att = rcopy(att, patt, pair_ssem.at[4], pair_rsem.at[4], mate)
    pair_att.start()
    up_other.wait_recv()
    up_both.start()
    windows(uh[1].astype(F32), umat4.at[1])
    up_mate.wait_recv()
    windows(uh[2].astype(F32), umat4.at[2])
    up_both.wait_recv()
    windows(uh[3].astype(F32), umat4.at[3])
    attt[:, 0:CELLS] = att[...].T
    pair_att.wait_recv()
    attt[:, CELLS : 2 * CELLS] = patt[...].T

    share_wait(st2, st_ssem.at[1], st_rsem.at[1], s)
    mean2, inverse2 = moments(st2)
    scale = 1.0 + mod[0:1, 0:W]
    shift = mod[0:1, W : 2 * W]
    gain = inverse2 * scale

    def act_of(ref):
        return silu((ref[...].astype(F32) - mean2) * inverse2 * scale + shift).astype(BF16)

    hats = (hid[...].astype(F32) - mean2) * inverse2
    hat[...] = hats
    shifted = hats * scale + shift
    sigma = jax.nn.sigmoid(shifted)
    act = (shifted * sigma).astype(BF16)
    actp[64:320, :] = act
    actt[0] = act.T
    pair_act = rcopy(actt.at[0], actt.at[2], pair_ssem.at[5], pair_rsem.at[5], mate)
    pair_act.start()
    hid_other.wait_recv()
    xact[...] = act_of(hx)
    actt[1] = xact[...].T
    pair_xact = rcopy(actt.at[1], actt.at[3], pair_ssem.at[7], pair_rsem.at[7], mate)
    pair_xact.start()

    through = back[...] * sigma * (1.0 + shifted * (1.0 - sigma)) * scale
    thr[...] = through
    st3[s] = pack(
        jnp.sum(through, axis=0, keepdims=True),
        jnp.sum(through * hats, axis=0, keepdims=True),
    )
    share_start(st3, st_ssem.at[2], st_rsem.at[2], s)

    actp[pl.ds(pl.multiple_of(320 * (1 - xl), 64), 64), :] = xact[
        pl.ds(pl.multiple_of(192 * xl, 64), 64), :
    ]
    edge = pl.ds(pl.multiple_of(320 * xl, 64), 64)

    @pl.when(has_far)
    def _():
        hid_far.wait_recv()
        actp[edge, :] = act_of(hfar)

    @pl.when(jnp.logical_not(has_far))
    def _():
        actp[edge, :] = blank

    windows(actp[...].astype(F32), amat)
    pair_act.wait_recv()
    pair_xact.wait_recv()

    def grad_copy(half, to):
        return rcopy(
            gst.at[pl.ds(pl.multiple_of(576 * to + 288 * core + 144 * half, 16), 144)],
            grecv.at[chip, pl.ds(144 * half, 144)],
            g_ssem.at[half, to],
            g_rsem.at[half, chip],
            {"dp": 2 * to + core},
        )

    def grad_step(j):
        p = lax.rem(chip + 1 + j, 9)
        a = p // 3
        b = lax.rem(p, 3)
        rows = pl.ds(pl.multiple_of(64 * (2 - a), 64), CELLS)
        lanes = pl.ds(pl.multiple_of(HALF * (2 - b), HALF), HALF)
        part = dot(actt[0], umat4[0, rows, lanes])
        for i in range(1, 4):
            part += dot(actt[i], umat4[i, rows, lanes])
        gst[pl.ds(pl.multiple_of(W * p, W), W), :] = part.astype(BF16)

        @pl.when((j >= 1) & (p >= 1) & (p - 1 != afar))
        def _():
            grad_copy(0, p - 1).start()

    loop(0, 9, grad_step)

    share_wait(st3, st_ssem.at[2], st_rsem.at[2], s)
    sums = group_sum(jnp.sum(st3[...], axis=0)) / 65536.0
    gf_ref[...] = (inverse2 * (thr[...] - unpack(sums) - hat[...] * unpack(sums, 4))).astype(BF16)
    pair_gf = rcopy(gf_ref, pgf, pair_ssem.at[6], pair_rsem.at[6], mate)
    pair_gf.start()
    gf_out = pltpu.make_async_copy(gf_ref, gf_hbm, lsem.at[7])
    gf_out.start()
    part = dot(attt[:, 0:CELLS], gf_ref[...])
    pair_gf.wait_recv()
    gost[...] = (part + dot(attt[:, CELLS : 2 * CELLS], pgf[...])).astype(BF16)

    def send_out(k):
        to = lax.rem(chip + k, 8)
        rcopy(
            gost.at[pl.ds(pl.multiple_of(64 * to + 32 * core, 32), 32)],
            gorecv.at[chip],
            o_ssem.at[to],
            o_rsem.at[chip],
            {"dp": 2 * to + core},
        ).start()

    loop(1, 8, send_out)

    def near_chips(fn):
        def go(k):
            to = lax.rem(chip + k, 8)

            @pl.when(to != afar)
            def _():
                fn(to)

        loop(1, 8, go)

    near_chips(lambda to: grad_copy(1, to).start())
    rows_afar = gst[pl.ds(pl.multiple_of(576 * afar + 288 * core, 32), 288), :]
    wide32[...] = rows_afar.astype(F32)
    pack32[...] = jnp.zeros_like(pack32)
    for i in range(8):
        for q in range(2):
            pack32[pl.ds(q, 36, stride=2), :] = wide32[36 * i : 36 * i + 36, 128 * q : 128 * q + 128]
        zpiece[i] = pack32[...].astype(BF16)

    def z_copy(k):
        h = lax.rem(z + k, 8)
        return rcopy(
            zpiece.at[h], zrecv.at[z], z_ssem.at[h], z_rsem.at[z], {"space": 2 * h + xl}
        )

    loop(1, 8, lambda k: z_copy(k).start())
    zrecv[z] = zpiece[z]

    thr[...] = jnp.zeros_like(thr)

    def conv_step(a):
        thr[...] += dot(
            amat[pl.ds(pl.multiple_of(64 * a, 64), CELLS), :],
            wconv[pl.ds(pl.multiple_of(3 * W * a, W), 3 * W), :],
        )

    loop(0, 3, conv_step)
    out_ref[...] = thr[...].astype(BF16)
    out_out = pltpu.make_async_copy(out_ref, out_hbm, lsem.at[8])
    out_out.start()

    def second(half):
        def take_grad(frm):
            part = grecv.at[frm, pl.ds(144 * half, 144)]
            rcopy(part, part, g_ssem.at[half, frm], g_rsem.at[half, frm], mate).wait_recv()

        near_chips(take_grad)
        grecv[chip, 144 * half : 144 * half + 144] = gst[
            pl.ds(pl.multiple_of(576 * chip + 288 * core + 144 * half, 16), 144), :
        ]
        sum2[...] = jnp.sum(grecv[:, 144 * half : 144 * half + 144].astype(F32), axis=0)
        for i in range(8):
            t = 8 * half + i
            for q in range(2):
                piece32[pl.ds(q, 18, stride=2), :] = sum2[
                    18 * i : 18 * i + 18, 128 * q : 128 * q + 128
                ]
            piece[t] = piece32[...].astype(BF16)

        def send_piece(i):
            t = 8 * half + i

            @pl.when(t != s)
            def _():
                rcopy(piece.at[t], precv.at[s], p_ssem.at[t], p_rsem.at[s], {"space": t}).start()

            @pl.when(t == s)
            def _():
                precv[s] = piece[s]

        loop(0, 8, send_piece)

    piece32[...] = jnp.zeros_like(piece32)
    grecv[afar] = jnp.zeros((288, HALF), BF16)
    second(0)

    def take_z(k):
        h = lax.rem(z + k, 8)
        rcopy(zpiece.at[h], zrecv.at[h], z_ssem.at[h], z_rsem.at[h], other).wait_recv()

    loop(1, 8, take_z)
    pack32[...] = jnp.sum(zrecv[...].astype(F32), axis=0)

    def far_copy(side):
        return rcopy(
            fpiece.at[side], frecv.at[xl], f_ssem.at[side], f_rsem.at[xl],
            {"dp": 2 * afar + core, "space": 2 * z + side},
        )

    for side in range(2):
        piece32[0:36, :] = pack32[36 * side : 36 * side + 36, :]
        fpiece[side] = piece32[...].astype(BF16)
        far_copy(side).start()

    def take_out(k):
        frm = lax.rem(chip + k, 8)
        rcopy(gorecv.at[frm], gorecv.at[frm], o_ssem.at[frm], o_rsem.at[frm], mate).wait_recv()

    loop(1, 8, take_out)
    gorecv[chip] = gost[pl.ds(pl.multiple_of(64 * chip + 32 * core, 32), 32), :]
    out_sum = jnp.sum(gorecv[...].astype(F32), axis=0)
    for t in range(N):
        opiece[t] = pack(out_sum[2 * t : 2 * t + 1], out_sum[2 * t + 1 : 2 * t + 2])

    def send_opiece(k):
        t = lax.rem(s + k, N)
        rcopy(opiece.at[t], oprecv.at[s], op_ssem.at[k], op_rsem.at[s], {"space": t}).start()

    loop(1, N, send_opiece)
    oprecv[s] = opiece[s]
    second(1)

    for p in range(8):
        forward(p).wait_send()
        if p:
            kv_copy(p).wait_send()
            q_copy(p).wait_send()
            rcopy(ats.at[p], atr.at[0], at_ssem.at[p], at_rsem.at[0], other).wait_send()

    def chips_sent(k):
        to = lax.rem(chip + k, 8)
        rcopy(gorecv.at[to], gorecv.at[to], o_ssem.at[to], o_rsem.at[to], mate).wait_send()
        z_copy(k).wait_send()

        @pl.when(to != afar)
        def _():
            grad_copy(0, to).wait_send()
            grad_copy(1, to).wait_send()

    loop(1, 8, chips_sent)
    far_copy(0).wait_send()
    far_copy(1).wait_send()
    for copy in (up_mate, up_other, up_both, hid_other, pair_att, pair_act, pair_xact, pair_gf):
        copy.wait_send()

    @pl.when(s > 0)
    def _():
        up_top.wait_send()

    @pl.when(s < N - 1)
    def _():
        up_bottom.wait_send()

    @pl.when(has_far)
    def _():
        hid_far.wait_send()

    gf_out.wait()
    out_out.wait()

    def take_pieces(k):
        t = lax.rem(s + k, N)
        g = rcopy(piece.at[t], precv.at[t], p_ssem.at[t], p_rsem.at[t], {"space": t})
        g.wait_send()
        g.wait_recv()

    loop(1, N, take_pieces)
    for side in range(2):
        rcopy(
            fpiece.at[side], frecv.at[side], f_ssem.at[side], f_rsem.at[side], other
        ).wait_recv()
        total = precv[side].astype(F32) + frecv[side].astype(F32)
        for i in range(1, 8):
            total += precv[2 * i + side].astype(F32)
        piece32[...] = total
        for q in range(2):
            gc_ref[pl.ds(2 * side + q, 18, stride=4), :] = piece32[pl.ds(q, 18, stride=2), :]

    def take_opieces(k):
        t = lax.rem(s + k, N)
        o = rcopy(opiece.at[t], oprecv.at[t], op_ssem.at[k], op_rsem.at[t], {"space": t})
        o.wait_send()
        o.wait_recv()

    loop(1, N, take_opieces)
    go_ref[...] = jnp.sum(oprecv[...], axis=0)


def hand_on(*refs):
    ins, outs, kept, sem = refs[:4], refs[4:8], refs[8:12], refs[12]
    first = [pltpu.make_async_copy(a, b, sem.at[0, i]) for i, (a, b) in enumerate(zip(ins, kept))]
    then = [pltpu.make_async_copy(a, b, sem.at[1, i]) for i, (a, b) in enumerate(zip(kept, outs))]
    for copy in first:
        copy.start()
    for came, goes in zip(first, then):
        came.wait()
        goes.start()
    for copy in then:
        copy.wait()


def on_device(features, timestep, w_time, w_emb, w_qkv, w_out, w_conv, upstream):
    vmem = pl.BlockSpec(memory_space=pltpu.VMEM)
    hbm = pl.BlockSpec(memory_space=pl.ANY)
    V = pltpu.VMEM
    dma = pltpu.SemaphoreType.DMA
    scratch = [
        V((CELLS, W), BF16), V((TFEAT, W), BF16), V((W, 2 * W), BF16), V((W, 3 * W), BF16),
        V((W, W), BF16), V((9 * W, W), BF16),
        V((N, 8, 128), F32), V((N, 8, 128), F32), V((N, 8, 128), F32),
        V((8, CELLS, 128), BF16), V((8, 128, 128), BF16), V((N, CELLS, 128), BF16), V((8, 128, 128), BF16),
        V((8, CELLS, 128), BF16), V((N, CELLS, 128), BF16), V((8, CELLS, 128), F32), V((8, CELLS, 128), F32),
        V((2, 4, CELLS, CELLS), F32), V((8, 128, 128), BF16), V((8, 128, 128), BF16), V((CELLS, W), BF16),
        V((384, W), BF16), V((384, HALF), BF16), V((4, 384, HALF), BF16), V((384, 3 * W), BF16),
        V((4, 384, 3 * HALF), BF16),
        V((CELLS, W), BF16), V((CELLS, W), BF16), V((64, W), BF16), V((384, W), BF16), V((CELLS, W), BF16),
        V((384, 3 * W), BF16), V((CELLS, W), BF16), V((CELLS, W), BF16), V((CELLS, W), BF16),
        V((4, W, CELLS), BF16), V((W, 2 * CELLS), BF16),
        V((CELLS, W), BF16), V((CELLS, W), F32), V((CELLS, W), F32), V((CELLS, W), F32), V((CELLS, W), F32),
        V((8, 2 * W), F32),
        V((9 * W, HALF), BF16), V((8, 288, HALF), BF16), V((W, W), BF16), V((8, 32, W), BF16),
        V((144, HALF), F32), V((48, 128), F32), V((N, 48, 128), BF16), V((N, 48, 128), BF16),
        V((N, 8, 128), F32), V((N, 8, 128), F32),
        V((288, HALF), F32), V((80, 128), F32), V((8, 80, 128), BF16), V((8, 80, 128), BF16),
        V((2, 48, 128), BF16), V((2, 48, 128), BF16),
        dma((9,)),
        dma((3, N)), dma((3, N)),
        dma((8,)), dma((N,)), dma((8,)), dma((8,)), dma((8,)), dma((8,)), dma((8,)),
        dma((3,)), dma((3,)), dma((8,)), dma((8,)),
        dma((2, 8)), dma((2, 8)), dma((8,)), dma((8,)), dma((N,)), dma((N,)), dma((N,)), dma((N,)),
        dma((8,)), dma((8,)), dma((2,)), dma((2,)),
    ]
    shapes = (
        jax.ShapeDtypeStruct((CELLS, W), BF16),
        jax.ShapeDtypeStruct((CELLS, W), BF16),
        jax.ShapeDtypeStruct((72, 128), F32),
        jax.ShapeDtypeStruct((8, 128), F32),
    )
    made = pl.pallas_call(
        kernel,
        out_shape=shapes,
        in_specs=[hbm, pl.BlockSpec(memory_space=pltpu.SMEM), hbm, hbm, hbm, hbm, hbm, hbm],
        out_specs=(hbm, hbm, vmem, vmem),
        scratch_shapes=scratch,
        compiler_params=pltpu.CompilerParams(
            collective_id=0, has_side_effects=True, vmem_limit_bytes=60 * 1024 * 1024
        ),
    )(
        features.reshape(CELLS, W), timestep, upstream.reshape(CELLS, W),
        w_time, w_emb, w_qkv, w_out, w_conv,
    )
    out, gf, gc, go = pl.pallas_call(
        hand_on,
        out_shape=shapes,
        in_specs=[hbm] * 4,
        out_specs=(hbm,) * 4,
        scratch_shapes=[V(shape.shape, shape.dtype) for shape in shapes] + [dma((2, 4))],
    )(*made)
    return (
        out.reshape(features.shape),
        gf.reshape(features.shape),
        gc.reshape(-1),
        go.reshape(-1),
    )


def solution(mesh):
    return jax.shard_map(
        on_device,
        mesh=mesh,
        in_specs=(
            P("dp", "space", None, None), P("dp"), P(), P(), P(), P(), P(),
            P("dp", "space", None, None),
        ),
        out_specs=(
            P("dp", "space", None, None), P("dp", "space", None, None),
            P(("dp", "space")), P(("dp", "space")),
        ),
        check_vma=False,
    )
```

```python
import functools
import math

import jax
import jax.numpy as jnp
from jax import lax
from jax.experimental import pallas as pl
from jax.experimental.pallas import tpu as pltpu
from jax.sharding import PartitionSpec as P

MESH = pl.DeviceIdType.MESH
F32 = jnp.float32
BF16 = jnp.bfloat16
EPS = 1e-05
LOG2E = 1.4426950408889634
TFEAT = 128
N = 16
CELLS = 256
W = 512
HALF = 256
NEAR = (0, 1, 7, 2, 6, 3, 5, 4)


def rcopy(src, dst, ssem, rsem, dev):
    return pltpu.make_async_remote_copy(
        src_ref=src, dst_ref=dst, send_sem=ssem, recv_sem=rsem, device_id=dev, device_id_type=MESH
    )


def loop(lo, hi, fn):
    def body(k, carry):
        fn(k)
        return carry

    lax.fori_loop(lo, hi, body, 0)


def far_first(i):
    return 8 + jnp.where(lax.rem(i, 2) == 1, i // 2, -(i // 2))


def share_start(buf, ssem, rsem, s):
    def go(i):
        k = far_first(i)
        t = lax.rem(s + k, N)
        rcopy(buf.at[s], buf.at[s], ssem.at[k], rsem.at[s], {"space": t}).start()

    loop(1, N, go)


def share_wait(buf, ssem, rsem, s):
    def go(k):
        t = lax.rem(s + k, N)
        copy = rcopy(buf.at[t], buf.at[t], ssem.at[k], rsem.at[t], {"space": t})
        copy.wait_send()
        copy.wait_recv()

    loop(1, N, go)


def group_sum(v):
    lane = lax.broadcasted_iota(jnp.int32, v.shape, 1)
    for k in (1, 2, 4, 8):
        v = v + jnp.where((lane & k) == 0, pltpu.roll(v, 128 - k, 1), pltpu.roll(v, k, 1))
    return v


def pack(a, b):
    return jnp.concatenate(
        [a[:, 128 * q : 128 * q + 128] for q in range(4)]
        + [b[:, 128 * q : 128 * q + 128] for q in range(4)],
        axis=0,
    )


def unpack(v, first=0):
    return jnp.concatenate([v[first + q : first + q + 1, :] for q in range(4)], axis=1)


def local_moments(values):
    mu = jnp.sum(values, axis=0, keepdims=True) / CELLS
    off = values - mu
    return pack(mu, jnp.sum(off * off, axis=0, keepdims=True))


def moments(buf):
    every = buf[...]
    total = jnp.sum(every, axis=0)
    mean = group_sum(total) / 256.0
    off = every - mean[None]
    spread = jnp.sum(off * off, axis=0) * CELLS + pltpu.roll(total, 4, 0)
    inverse = lax.rsqrt(group_sum(spread) / 65536.0 + EPS)
    return unpack(mean), unpack(inverse)


def dot(a, b):
    return jnp.dot(a, b, preferred_element_type=F32)


def dot_nt(a, b):
    return lax.dot_general(a, b, (((1,), (1,)), ((), ())), preferred_element_type=F32)


def exact_dot(v, w):
    high = v.astype(BF16)
    rest = v - high.astype(F32)
    mid = rest.astype(BF16)
    low = (rest - mid.astype(F32)).astype(BF16)
    return dot(high, w) + dot(mid, w) + dot(low, w)


def windows(v, dst):
    col = lax.broadcasted_iota(jnp.int32, v.shape, 0) & 63
    height, width = v.shape
    dst[:, 0:width] = jnp.where(col != 0, pltpu.roll(v, 1, 0), 0.0).astype(BF16)
    dst[:, width : 2 * width] = v.astype(BF16)
    dst[:, 2 * width : 3 * width] = jnp.where(col != 63, pltpu.roll(v, height - 1, 0), 0.0).astype(
        BF16
    )


def silu(v):
    return v * jax.nn.sigmoid(v)


def kernel(
    x_hbm, t_ref, up_hbm, wtime_hbm, wemb_hbm, wqkv_hbm, wout_hbm, wconv_hbm,
    out_hbm, gf_hbm, gc_ref, go_ref,
    x_ref, wtime, wemb, wqkv, wout, wconv,
    st1, st2, st3,
    kvs, qs, kvr, qr, qq, val, top, acc, score, ats, atr, att,
    upp, uo, uh, umat, umat4,
    hid, hx, hfar, actp, xact, amat, patt, gf_ref, pgf, actt, attt,
    out_ref, hat, zed, back, thr, mod,
    gst, grecv, gost, gorecv, sum2, piece32, piece, precv, opiece, oprecv,
    wide32, pack32, zpiece, zrecv, fpiece, frecv, owned,
    lsem,
    st_ssem, st_rsem,
    kv_ssem, kv_rsem, fw_ssem, q_ssem, q_rsem, at_ssem, at_rsem,
    halo_ssem, halo_rsem, pair_ssem, pair_rsem,
    g_ssem, g_rsem, o_ssem, o_rsem, p_ssem, p_rsem, op_ssem, op_rsem, z_ssem, z_rsem, f_ssem, f_rsem,
):
    d = lax.axis_index("dp")
    s = lax.axis_index("space")
    z = s // 2
    xl = lax.rem(s, 2)
    chip = d // 2
    core = lax.rem(d, 2)
    mate = {"dp": 2 * chip + 1 - core}
    other = {"space": 2 * z + 1 - xl}
    afar = 2 * lax.rem(chip // 2 + 2, 4) + 1 - lax.rem(chip, 2)

    loads = [
        pltpu.make_async_copy(a, b, lsem.at[i])
        for i, (a, b) in enumerate(
            (
                (x_hbm, x_ref),
                (wqkv_hbm, wqkv),
                (up_hbm, upp.at[pl.ds(64, CELLS)]),
                (wtime_hbm, wtime),
                (wemb_hbm, wemb),
                (wconv_hbm, wconv),
                (wout_hbm, wout),
            )
        )
    ]
    loads[0].start()
    loads[1].start()

    barrier = pltpu.get_barrier_semaphore()

    def greet(dev):
        pl.semaphore_signal(barrier, inc=1, device_id=dev, device_id_type=MESH)

    loop(1, N, lambda i: greet({"space": lax.rem(s + far_first(i), N)}))
    loop(1, 8, lambda k: greet({"dp": 2 * lax.rem(chip + k, 8) + core}))
    greet(mate)
    greet({"dp": 2 * afar + core, "space": 2 * z + 1 - xl})

    blank = jnp.zeros((64, W), BF16)

    @pl.when(s == 0)
    def _():
        upp[0:64, :] = blank

    @pl.when(s == N - 1)
    def _():
        upp[320:384, :] = blank

    loads[0].wait()
    st1[s] = local_moments(x_ref[...].astype(F32))
    for load in loads[2:]:
        load.start()
    pl.semaphore_wait(barrier, 15 + 7 + 1 + 1)
    share_start(st1, st_ssem.at[0], st_rsem.at[0], s)

    loads[2].wait()
    up_top = rcopy(
        upp.at[pl.ds(64, 64)], upp.at[pl.ds(320, 64)], halo_ssem.at[0], halo_rsem.at[0],
        {"space": jnp.maximum(s - 1, 0)},
    )
    up_bottom = rcopy(
        upp.at[pl.ds(256, 64)], upp.at[pl.ds(0, 64)], halo_ssem.at[1], halo_rsem.at[1],
        {"space": jnp.minimum(s + 1, N - 1)},
    )

    @pl.when(s > 0)
    def _():
        up_top.start()

    @pl.when(s < N - 1)
    def _():
        up_bottom.start()


    loads[1].wait()
    share_wait(st1, st_ssem.at[0], st_rsem.at[0], s)
    mean1, inverse1 = moments(st1)
    normed = ((x_ref[...].astype(F32) - mean1) * inverse1).astype(BF16)
    low_half = lax.broadcasted_iota(jnp.int32, (CELLS, 128), 1) < 64
    low_short = lax.broadcasted_iota(jnp.int32, (128, 128), 1) < 64
    for pair in range(4):
        q = dot(normed, wqkv[:, 128 * pair : 128 * pair + 128])
        q = q.astype(BF16).astype(F32) * 0.125
        turned = pltpu.roll(q, 64, 1)
        qs[2 * pair] = jnp.where(low_short, q[0:128], turned[128:256]).astype(BF16)
        qs[2 * pair + 1] = jnp.where(low_short, turned[0:128], q[128:256]).astype(BF16)

    def q_copy(p):
        h = lax.rem(z + NEAR[p], 8)
        slot = NEAR.index((8 - NEAR[p]) % 8)
        return rcopy(
            qs.at[h], qr.at[slot], q_ssem.at[p], q_rsem.at[slot], {"space": 2 * h + xl}
        )

    def kv_copy(p):
        h = lax.rem(z + NEAR[p], 8)
        slot = NEAR.index((8 - NEAR[p]) % 8)
        return rcopy(
            kvs.at[h], kvr.at[slot], kv_ssem.at[p], kv_rsem.at[slot], {"space": 2 * h + xl}
        )

    def forward(p):
        return rcopy(kvr.at[p], kvr.at[8 + p], fw_ssem.at[p], kv_rsem.at[8 + p], other)

    for p in range(1, 8):
        q_copy(p).start()
    for pair in range(4):
        k = dot(normed, wqkv[:, W + 128 * pair : W + 128 * pair + 128])
        v = dot(normed, wqkv[:, 2 * W + 128 * pair : 2 * W + 128 * pair + 128])
        kvs[2 * pair] = jnp.where(low_half, k, pltpu.roll(v, 64, 1)).astype(BF16)
        kvs[2 * pair + 1] = jnp.where(low_half, pltpu.roll(k, 64, 1), v).astype(BF16)
    for p in (1, 2):
        kv_copy(p).start()
    kvr[0] = kvs[z]
    qr[0] = qs[z]
    forward(0).start()

    loads[3].wait()
    loads[4].wait()
    spot = lax.broadcasted_iota(jnp.int32, (8, TFEAT), 1)
    nth = (spot & (TFEAT // 2 - 1)).astype(F32)
    angle = t_ref[0].astype(F32) * jnp.exp(-math.log(10000.0) * nth / (TFEAT // 2))
    embedded = exact_dot(jnp.where(spot < TFEAT // 2, jnp.cos(angle), jnp.sin(angle)), wtime[...])
    mod[...] = exact_dot(silu(embedded), wemb[...])

    @pl.when(s < N - 1)
    def _():
        up_top.wait_recv()

    @pl.when(s > 0)
    def _():
        up_bottom.wait_recv()

    uh[0] = upp[:, pl.ds(pl.multiple_of(HALF * xl, HALF), HALF)]
    uo[...] = upp[:, pl.ds(pl.multiple_of(HALF * (1 - xl), HALF), HALF)]
    up_mate = rcopy(uh.at[0], uh.at[2], pair_ssem.at[0], pair_rsem.at[0], mate)
    up_other = rcopy(uo, uh.at[1], pair_ssem.at[1], pair_rsem.at[1], other)
    up_both = rcopy(uh.at[1], uh.at[3], pair_ssem.at[2], pair_rsem.at[2], mate)
    up_mate.start()
    windows(upp[...].astype(F32), umat)
    windows(uh[0].astype(F32), umat4.at[0])
    loads[5].wait()
    loads[6].wait()
    back[...] = jnp.zeros_like(back)
    kv_copy(3).start()
    kv_copy(4).start()

    def back_step(p):
        a = p // 3
        b = lax.rem(p, 3)
        rows = pl.ds(pl.multiple_of(64 * (2 - a), 64), CELLS)
        lanes = pl.ds(pl.multiple_of(W * (2 - b), W), W)
        back[...] += dot_nt(umat[rows, lanes], wconv[pl.ds(pl.multiple_of(W * p, W), W), :])

    loop(0, 9, back_step)

    for p in range(1, 8):
        q_copy(NEAR.index((8 - NEAR[p]) % 8)).wait_recv()
    kv_copy(5).start()
    kv_copy(6).start()
    for p in range(8):
        q = qr[p].astype(F32)
        qq[p, 0:128, :] = jnp.where(low_short, q, 0.0).astype(BF16)
        qq[p, 128:256, :] = jnp.where(low_short, pltpu.roll(q, 64, 1), 0.0).astype(BF16)

    def take(p):
        if 1 <= p < 8:
            kv_copy(NEAR.index((8 - NEAR[p]) % 8)).wait_recv()
            forward(p).start()
        if p >= 8:
            forward(p - 8).wait_recv()
        val[p] = jnp.where(low_half, 1.0, kvr[p].astype(F32)).astype(BF16)

    def scores(i, slots, b):
        for j, p in enumerate(slots):
            score[b, j] = dot_nt(qq[i], kvr[p])

    def attend(i, slots, b, first, last):
        high = None
        for j in range(len(slots)):
            part = jnp.maximum(score[b, j, :, 0:128], score[b, j, :, 128:256])
            high = part if high is None else jnp.maximum(high, part)
        high = jnp.max(high, axis=1, keepdims=True) * LOG2E
        if not first:
            before = top[i]
            high = jnp.maximum(before, high)
        else:
            high = jnp.broadcast_to(high, (CELLS, 128))
        wide = jnp.concatenate([high, high], axis=1)
        total = None
        for j, p in enumerate(slots):
            mixed = dot(jnp.exp2(score[b, j] * LOG2E - wide).astype(BF16), val[p])
            total = mixed if total is None else total + mixed
        if not first:
            total = total + acc[i] * jnp.exp2(before - high)
        if not last:
            top[i] = high
            acc[i] = total
        return total

    def finish(total):
        ratio = total / pltpu.roll(total, 64, 1)
        return jnp.where(low_short, pltpu.roll(ratio[0:128], 64, 1), ratio[128:256]).astype(BF16)

    def go(*slots):
        first, last = 0 in slots, 15 in slots

        def use(i, b):
            total = attend(i, slots, b, first, last)
            if last:
                ats[i] = finish(total)

                @pl.when(i > 0)
                def _():
                    away = jnp.where(lax.rem(i, 2) == 1, (i + 1) // 2, 8 - i // 2)
                    there = 2 * lax.rem(z + away, 8) + xl
                    rcopy(
                        ats.at[i], atr.at[z], at_ssem.at[i], at_rsem.at[z], {"space": there}
                    ).start()

        def turn(k):
            return 7 - k if last else k

        def step(m):
            k = 2 * m
            scores(turn(k + 1), slots, 1)
            use(turn(k), 0)
            scores(turn(jnp.minimum(k + 2, 7)), slots, 0)
            use(turn(k + 1), 1)

        scores(turn(0), slots, 0)
        loop(0, 4, step)

    take(0)
    take(8)
    take(1)
    take(2)
    kv_copy(7).start()
    go(0, 8, 1, 2)
    take(3)
    take(4)
    take(9)
    take(10)
    go(3, 4, 9, 10)
    take(5)
    take(6)
    take(11)
    take(12)
    go(5, 6, 11, 12)
    for p in (7, 13, 14, 15):
        take(p)
    up_other.start()
    go(7, 13, 14, 15)
    atr[z] = ats[0]

    for k in range(1, 8):
        h = lax.rem(z + k, 8)
        rcopy(ats.at[k], atr.at[h], at_ssem.at[k], at_rsem.at[h], other).wait_recv()
    for pair in range(4):
        first = atr[2 * pair].astype(F32)
        second = atr[2 * pair + 1].astype(F32)
        lanes = slice(128 * pair, 128 * pair + 128)
        att[0:128, lanes] = jnp.where(low_short, first, pltpu.roll(second, 64, 1)).astype(BF16)
        att[128:256, lanes] = jnp.where(low_short, pltpu.roll(first, 64, 1), second).astype(BF16)

    hidden = (x_ref[...].astype(F32) + dot(att[...], wout[...])).astype(BF16)
    hid[...] = hidden
    hidden = hidden.astype(F32)
    st2[s] = local_moments(hidden)
    share_start(st2, st_ssem.at[1], st_rsem.at[1], s)
    far = s - 1 + 2 * xl
    has_far = (far >= 0) & (far < N)
    hid_far = rcopy(
        hid.at[pl.ds(pl.multiple_of(192 * xl, 64), 64)], hfar, halo_ssem.at[2], halo_rsem.at[2],
        {"space": jnp.clip(far, 0, N - 1)},
    )

    @pl.when(has_far)
    def _():
        hid_far.start()

    hid_other = rcopy(hid, hx, pair_ssem.at[3], pair_rsem.at[3], other)
    hid_other.start()
    pair_att = rcopy(att, patt, pair_ssem.at[4], pair_rsem.at[4], mate)
    pair_att.start()
    up_other.wait_recv()
    up_both.start()
    windows(uh[1].astype(F32), umat4.at[1])
    up_mate.wait_recv()
    windows(uh[2].astype(F32), umat4.at[2])
    up_both.wait_recv()
    windows(uh[3].astype(F32), umat4.at[3])
    attt[:, 0:CELLS] = att[...].T
    pair_att.wait_recv()
    attt[:, CELLS : 2 * CELLS] = patt[...].T

    share_wait(st2, st_ssem.at[1], st_rsem.at[1], s)
    mean2, inverse2 = moments(st2)
    scale = 1.0 + mod[0:1, 0:W]
    shift = mod[0:1, W : 2 * W]
    gain = inverse2 * scale

    def act_of(ref):
        return silu((ref[...].astype(F32) - mean2) * inverse2 * scale + shift).astype(BF16)

    hats = (hid[...].astype(F32) - mean2) * inverse2
    hat[...] = hats
    shifted = hats * scale + shift
    sigma = jax.nn.sigmoid(shifted)
    act = (shifted * sigma).astype(BF16)
    actp[64:320, :] = act
    actt[0] = act.T
    pair_act = rcopy(actt.at[0], actt.at[2], pair_ssem.at[5], pair_rsem.at[5], mate)
    pair_act.start()
    hid_other.wait_recv()
    xact[...] = act_of(hx)
    actt[1] = xact[...].T
    pair_xact = rcopy(actt.at[1], actt.at[3], pair_ssem.at[7], pair_rsem.at[7], mate)
    pair_xact.start()

    through = back[...] * sigma * (1.0 + shifted * (1.0 - sigma)) * scale
    thr[...] = through
    st3[s] = pack(
        jnp.sum(through, axis=0, keepdims=True),
        jnp.sum(through * hats, axis=0, keepdims=True),
    )
    share_start(st3, st_ssem.at[2], st_rsem.at[2], s)

    actp[pl.ds(pl.multiple_of(320 * (1 - xl), 64), 64), :] = xact[
        pl.ds(pl.multiple_of(192 * xl, 64), 64), :
    ]
    edge = pl.ds(pl.multiple_of(320 * xl, 64), 64)

    @pl.when(has_far)
    def _():
        hid_far.wait_recv()
        actp[edge, :] = act_of(hfar)

    @pl.when(jnp.logical_not(has_far))
    def _():
        actp[edge, :] = blank

    windows(actp[...].astype(F32), amat)
    pair_act.wait_recv()
    pair_xact.wait_recv()

    def grad_copy(half, to):
        return rcopy(
            gst.at[pl.ds(pl.multiple_of(576 * to + 288 * core + 144 * half, 16), 144)],
            grecv.at[chip, pl.ds(144 * half, 144)],
            g_ssem.at[half, to],
            g_rsem.at[half, chip],
            {"dp": 2 * to + core},
        )

    def grad_step(j):
        p = lax.rem(chip + 1 + j, 9)
        a = p // 3
        b = lax.rem(p, 3)
        rows = pl.ds(pl.multiple_of(64 * (2 - a), 64), CELLS)
        lanes = pl.ds(pl.multiple_of(HALF * (2 - b), HALF), HALF)
        part = dot(actt[0], umat4[0, rows, lanes])
        for i in range(1, 4):
            part += dot(actt[i], umat4[i, rows, lanes])
        gst[pl.ds(pl.multiple_of(W * p, W), W), :] = part.astype(BF16)

        @pl.when((j >= 1) & (p >= 1) & (p - 1 != afar))
        def _():
            grad_copy(0, p - 1).start()

    loop(0, 9, grad_step)

    share_wait(st3, st_ssem.at[2], st_rsem.at[2], s)
    sums = group_sum(jnp.sum(st3[...], axis=0)) / 65536.0
    gf_ref[...] = (inverse2 * (thr[...] - unpack(sums) - hat[...] * unpack(sums, 4))).astype(BF16)
    pair_gf = rcopy(gf_ref, pgf, pair_ssem.at[6], pair_rsem.at[6], mate)
    pair_gf.start()
    gf_out = pltpu.make_async_copy(gf_ref, gf_hbm, lsem.at[7])
    gf_out.start()
    part = dot(attt[:, 0:CELLS], gf_ref[...])
    pair_gf.wait_recv()
    gost[...] = (part + dot(attt[:, CELLS : 2 * CELLS], pgf[...])).astype(BF16)

    def send_out(k):
        to = lax.rem(chip + k, 8)
        rcopy(
            gost.at[pl.ds(pl.multiple_of(64 * to + 32 * core, 32), 32)],
            gorecv.at[chip],
            o_ssem.at[to],
            o_rsem.at[chip],
            {"dp": 2 * to + core},
        ).start()

    loop(1, 8, send_out)

    def near_chips(fn):
        def go(k):
            to = lax.rem(chip + k, 8)

            @pl.when(to != afar)
            def _():
                fn(to)

        loop(1, 8, go)

    near_chips(lambda to: grad_copy(1, to).start())
    rows_afar = gst[pl.ds(pl.multiple_of(576 * afar + 288 * core, 32), 288), :]
    wide32[0:288, :] = rows_afar.astype(F32)
    pack32[...] = jnp.zeros_like(pack32)
    for i in range(8):
        for q in range(2):
            pack32[pl.ds(q, 36, stride=2), :] = wide32[36 * i : 36 * i + 36, 128 * q : 128 * q + 128]
        zpiece[i] = pack32[0:80, :].astype(BF16)

    def z_copy(k):
        h = lax.rem(z + k, 8)
        return rcopy(
            zpiece.at[h], zrecv.at[z], z_ssem.at[h], z_rsem.at[z], {"space": 2 * h + xl}
        )

    loop(1, 8, lambda k: z_copy(k).start())
    zrecv[z] = zpiece[z]

    thr[...] = jnp.zeros_like(thr)

    def conv_step(a):
        thr[...] += dot(
            amat[pl.ds(pl.multiple_of(64 * a, 64), CELLS), :],
            wconv[pl.ds(pl.multiple_of(3 * W * a, W), 3 * W), :],
        )

    loop(0, 3, conv_step)
    out_ref[...] = thr[...].astype(BF16)
    out_out = pltpu.make_async_copy(out_ref, out_hbm, lsem.at[8])
    out_out.start()

    def second(half):
        def take_grad(frm):
            part = grecv.at[frm, pl.ds(144 * half, 144)]
            rcopy(part, part, g_ssem.at[half, frm], g_rsem.at[half, frm], mate).wait_recv()

        near_chips(take_grad)
        grecv[chip, 144 * half : 144 * half + 144] = gst[
            pl.ds(pl.multiple_of(576 * chip + 288 * core + 144 * half, 16), 144), :
        ]
        sum2[0:144, :] = jnp.sum(grecv[:, 144 * half : 144 * half + 144].astype(F32), axis=0)
        for i in range(8):
            t = 8 * half + i
            for q in range(2):
                piece32[pl.ds(q, 18, stride=2), :] = sum2[
                    18 * i : 18 * i + 18, 128 * q : 128 * q + 128
                ]
            piece[t] = piece32[...].astype(BF16)

        def send_piece(i):
            t = 8 * half + i

            @pl.when(t != s)
            def _():
                rcopy(piece.at[t], precv.at[s], p_ssem.at[t], p_rsem.at[s], {"space": t}).start()

            @pl.when(t == s)
            def _():
                precv[s] = piece[s]

        loop(0, 8, send_piece)

    piece32[...] = jnp.zeros_like(piece32)
    grecv[afar] = jnp.zeros((288, HALF), BF16)
    second(0)

    def take_z(k):
        h = lax.rem(z + k, 8)
        rcopy(zpiece.at[h], zrecv.at[h], z_ssem.at[h], z_rsem.at[h], other).wait_recv()

    loop(1, 8, take_z)
    pack32[0:80, :] = jnp.sum(zrecv[...].astype(F32), axis=0)

    def far_copy(side):
        return rcopy(
            fpiece.at[side], frecv.at[xl], f_ssem.at[side], f_rsem.at[xl],
            {"dp": 2 * afar + core, "space": 2 * z + side},
        )

    for side in range(2):
        piece32[0:36, :] = pack32[36 * side : 36 * side + 36, :]
        fpiece[side] = piece32[...].astype(BF16)
        far_copy(side).start()

    def take_out(k):
        frm = lax.rem(chip + k, 8)
        rcopy(gorecv.at[frm], gorecv.at[frm], o_ssem.at[frm], o_rsem.at[frm], mate).wait_recv()

    loop(1, 8, take_out)
    gorecv[chip] = gost[pl.ds(pl.multiple_of(64 * chip + 32 * core, 32), 32), :]
    out_sum = jnp.sum(gorecv[...].astype(F32), axis=0)
    for t in range(N):
        opiece[t] = pack(out_sum[2 * t : 2 * t + 1], out_sum[2 * t + 1 : 2 * t + 2])

    def send_opiece(k):
        t = lax.rem(s + k, N)
        rcopy(opiece.at[t], oprecv.at[s], op_ssem.at[k], op_rsem.at[s], {"space": t}).start()

    loop(1, N, send_opiece)
    oprecv[s] = opiece[s]
    second(1)

    for p in range(8):
        forward(p).wait_send()
        if p:
            kv_copy(p).wait_send()
            q_copy(p).wait_send()
            rcopy(ats.at[p], atr.at[0], at_ssem.at[p], at_rsem.at[0], other).wait_send()

    def chips_sent(k):
        to = lax.rem(chip + k, 8)
        rcopy(gorecv.at[to], gorecv.at[to], o_ssem.at[to], o_rsem.at[to], mate).wait_send()
        z_copy(k).wait_send()

        @pl.when(to != afar)
        def _():
            grad_copy(0, to).wait_send()
            grad_copy(1, to).wait_send()

    loop(1, 8, chips_sent)
    far_copy(0).wait_send()
    far_copy(1).wait_send()
    for copy in (up_mate, up_other, up_both, hid_other, pair_att, pair_act, pair_xact, pair_gf):
        copy.wait_send()

    @pl.when(s > 0)
    def _():
        up_top.wait_send()

    @pl.when(s < N - 1)
    def _():
        up_bottom.wait_send()

    @pl.when(has_far)
    def _():
        hid_far.wait_send()

    gf_out.wait()
    out_out.wait()

    def take_pieces(k):
        t = lax.rem(s + k, N)
        g = rcopy(piece.at[t], precv.at[t], p_ssem.at[t], p_rsem.at[t], {"space": t})
        g.wait_send()
        g.wait_recv()

    loop(1, N, take_pieces)
    for side in range(2):
        rcopy(
            fpiece.at[side], frecv.at[side], f_ssem.at[side], f_rsem.at[side], other
        ).wait_recv()
        total = precv[side].astype(F32) + frecv[side].astype(F32)
        for i in range(1, 8):
            total += precv[2 * i + side].astype(F32)
        piece32[...] = total
        for q in range(2):
            owned[pl.ds(2 * side + q, 18, stride=4), :] = piece32[pl.ds(q, 18, stride=2), :]

    gc_ref[...] = owned[0:72, :]

    def take_opieces(k):
        t = lax.rem(s + k, N)
        o = rcopy(opiece.at[t], oprecv.at[t], op_ssem.at[k], op_rsem.at[t], {"space": t})
        o.wait_send()
        o.wait_recv()

    loop(1, N, take_opieces)
    go_ref[...] = jnp.sum(oprecv[...], axis=0)


def hand_on(*refs):
    ins, outs, kept, sem = refs[:4], refs[4:8], refs[8:12], refs[12]
    first = [pltpu.make_async_copy(a, b, sem.at[0, i]) for i, (a, b) in enumerate(zip(ins, kept))]
    then = [pltpu.make_async_copy(a, b, sem.at[1, i]) for i, (a, b) in enumerate(zip(kept, outs))]
    for copy in first:
        copy.start()
    for came, goes in zip(first, then):
        came.wait()
        goes.start()
    for copy in then:
        copy.wait()


def on_device(features, timestep, w_time, w_emb, w_qkv, w_out, w_conv, upstream):
    vmem = pl.BlockSpec(memory_space=pltpu.VMEM)
    hbm = pl.BlockSpec(memory_space=pl.ANY)
    V = pltpu.VMEM
    dma = pltpu.SemaphoreType.DMA
    scratch = [
        V((CELLS, W), BF16), V((TFEAT, W), BF16), V((W, 2 * W), BF16), V((W, 3 * W), BF16),
        V((W, W), BF16), V((9 * W, W), BF16),
        V((N, 8, 128), F32), V((N, 8, 128), F32), V((N, 8, 128), F32),
        V((8, CELLS, 128), BF16), V((8, 128, 128), BF16), V((N, CELLS, 128), BF16), V((8, 128, 128), BF16),
        V((8, CELLS, 128), BF16), V((N, CELLS, 128), BF16), V((8, CELLS, 128), F32), V((8, CELLS, 128), F32),
        V((2, 4, CELLS, CELLS), F32), V((8, 128, 128), BF16), V((8, 128, 128), BF16), V((CELLS, W), BF16),
        V((384, W), BF16), V((384, HALF), BF16), V((4, 384, HALF), BF16), V((384, 3 * W), BF16),
        V((4, 384, 3 * HALF), BF16),
        V((CELLS, W), BF16), V((CELLS, W), BF16), V((64, W), BF16), V((384, W), BF16), V((CELLS, W), BF16),
        V((384, 3 * W), BF16), V((CELLS, W), BF16), V((CELLS, W), BF16), V((CELLS, W), BF16),
        V((4, W, CELLS), BF16), V((W, 2 * CELLS), BF16),
        V((CELLS, W), BF16), V((CELLS, W), F32), V((CELLS, W), F32), V((CELLS, W), F32), V((CELLS, W), F32),
        V((8, 2 * W), F32),
        V((9 * W, HALF), BF16), V((8, 288, HALF), BF16), V((W, W), BF16), V((8, 32, W), BF16),
        V((152, HALF), F32), V((48, 128), F32), V((N, 48, 128), BF16), V((N, 48, 128), BF16),
        V((N, 8, 128), F32), V((N, 8, 128), F32),
        V((296, HALF), F32), V((88, 128), F32), V((8, 80, 128), BF16), V((8, 80, 128), BF16),
        V((2, 48, 128), BF16), V((2, 48, 128), BF16), V((104, 128), F32),
        dma((9,)),
        dma((3, N)), dma((3, N)),
        dma((8,)), dma((N,)), dma((8,)), dma((8,)), dma((8,)), dma((8,)), dma((8,)),
        dma((3,)), dma((3,)), dma((8,)), dma((8,)),
        dma((2, 8)), dma((2, 8)), dma((8,)), dma((8,)), dma((N,)), dma((N,)), dma((N,)), dma((N,)),
        dma((8,)), dma((8,)), dma((2,)), dma((2,)),
    ]
    shapes = (
        jax.ShapeDtypeStruct((CELLS, W), BF16),
        jax.ShapeDtypeStruct((CELLS, W), BF16),
        jax.ShapeDtypeStruct((72, 128), F32),
        jax.ShapeDtypeStruct((8, 128), F32),
    )
    made = pl.pallas_call(
        kernel,
        out_shape=shapes,
        in_specs=[hbm, pl.BlockSpec(memory_space=pltpu.SMEM), hbm, hbm, hbm, hbm, hbm, hbm],
        out_specs=(hbm, hbm, vmem, vmem),
        scratch_shapes=scratch,
        compiler_params=pltpu.CompilerParams(
            collective_id=0, has_side_effects=True, vmem_limit_bytes=60 * 1024 * 1024
        ),
    )(
        features.reshape(CELLS, W), timestep, upstream.reshape(CELLS, W),
        w_time, w_emb, w_qkv, w_out, w_conv,
    )
    out, gf, gc, go = pl.pallas_call(
        hand_on,
        out_shape=shapes,
        in_specs=[hbm] * 4,
        out_specs=(hbm,) * 4,
        scratch_shapes=[V(shape.shape, shape.dtype) for shape in shapes] + [dma((2, 4))],
    )(*made)
    return (
        out.reshape(features.shape),
        gf.reshape(features.shape),
        gc.reshape(-1),
        go.reshape(-1),
    )


def solution(mesh):
    return jax.shard_map(
        on_device,
        mesh=mesh,
        in_specs=(
            P("dp", "space", None, None), P("dp"), P(), P(), P(), P(), P(),
            P("dp", "space", None, None),
        ),
        out_specs=(
            P("dp", "space", None, None), P("dp", "space", None, None),
            P(("dp", "space")), P(("dp", "space")),
        ),
        check_vma=False,
    )
```
